256 devices in a mesh: ctx: 32 (over z, y_lo, core), tp: 8 (over y_hi, x).
Axes of the slice: x: 4, y: 4 (y_hi: 2, y_lo: 2; y = y_hi * 2 + y_lo), z: 8, core: 2. Of those that a mesh axis runs over, the one named last changes fastest.
Arguments:
- query_in: bfloat16 [8192, 8192], P('ctx', 'tp'), may hold values from -6 to 6
- key_in: bfloat16 [8192, 8192], P('ctx', 'tp'), may hold values from -6 to 6
- value_in: bfloat16 [8192, 8192], P('ctx', 'tp'), may hold values from -6 to 6
- cotangent: bfloat16 [8192, 8192], P('ctx', 'tp'), may hold values from -6 to 6
- short_weight: float32 [3, 3, 8192], P(None, None, 'tp'), may hold values from -3 to 3
- long_filter: bfloat16 [8192, 8192], P('ctx', 'tp'), may hold values from -1.5 to 1.5
Outputs:
- block_out: bfloat16 [8192, 8192], P('ctx', 'tp')
- grad_query: bfloat16 [8192, 8192], P('ctx', 'tp')
- grad_key: bfloat16 [8192, 8192], P('ctx', 'tp')
- grad_value: bfloat16 [8192, 8192], P('ctx', 'tp')
- grad_short: float32 [3, 3, 8192], P(None, None, 'tp')
- grad_filter: bfloat16 [8192, 8192], P('ctx', 'tp')
The draws below stay inside these ranges and needn't reach their ends.
All inputs are finite; a program needn't handle non-finite values.
Results may differ from the reference program's by a relative error of at most 0.025.
Values may be sent and summed in bfloat16 or wider, within the bound.
No kernel may reach another device: no remote copies, remote signals or barrier semaphores. Data moves between devices by JAX's collectives and lax.ppermute only.
A program may use at most 64 MiB of HBM per device.

```python
import math
import jax
import jax.numpy as jnp
from jax import lax

D = 8192
KS = 3
S = 128
L = 8192


def draw_cotangent(key, part):
    key = jax.random.fold_in(key, 23)
    noise_key = jax.random.fold_in(key, 0)
    position = jnp.arange(L, dtype=jnp.float32)[:, None] / L
    noise = jnp.clip(jax.random.normal(noise_key, (L, D), jnp.float32), -4.0, 4.0)
    result = noise * (0.5 + position)
    return jnp.clip(result, -6.0, 6.0).astype(jnp.bfloat16)


def draw_long_filter(key, part):
    key = jax.random.fold_in(key, 11)
    chooser, slow_key, fast_key, noise_key = jax.random.split(key, 4)
    lowest = math.log(0.1 / L)
    middle = math.log(2.0 / L)
    highest = math.log(0.05)
    slow_rates = jnp.exp(lowest + (middle - lowest) * jax.random.uniform(slow_key, (1, D), jnp.float32))
    fast_rates = jnp.exp(middle + (highest - middle) * jax.random.uniform(fast_key, (1, D), jnp.float32))
    portion = 0.5
    picked = jax.random.uniform(chooser, (1, D), jnp.float32) < portion
    rates = jnp.where(picked, slow_rates, fast_rates)
    position = jnp.arange(L, dtype=jnp.float32)[:, None]
    envelope = jnp.exp(-rates * position) * jnp.sqrt(-jnp.expm1(-2.0 * rates))
    noise = jnp.clip(jax.random.normal(noise_key, (L, D), jnp.float32), -4.0, 4.0)
    return jnp.clip(noise * envelope, -1.5, 1.5).astype(jnp.bfloat16)


def shard_levels(rng, shape, pieces, low, top_value):
    gain = 1.0
    for dim, blocks in pieces:
        draws = jax.random.uniform(jax.random.fold_in(jax.random.fold_in(rng, 6), dim), (blocks,), jnp.float32, low / len(pieces), top_value / len(pieces))
        gain = gain * jnp.repeat(jnp.exp(draws), shape[dim] // blocks).reshape((-1,) + (1,) * (len(shape) - 1 - dim))
    return gain


def bell_draw(key, dims, deviation, limit, cuts=(), kind=jnp.bfloat16):
    drawn = jax.random.normal(key, dims, jnp.float32) * deviation
    if len(cuts) > 0:
        drawn = shard_levels(key, dims, cuts, -0.22, 0.18) * drawn
    return jnp.clip(drawn, min=-limit, max=limit).astype(kind)


def setup_inputs(seed: int = 0) -> dict:
    seeds = jax.random.split(jax.random.key(seed), 7)
    query_in = bell_draw(seeds[0], (L, D), 1.0, 6.0, ((0, 32), (1, 8)))
    key_in = bell_draw(seeds[1], (L, D), 1.0, 6.0, ((0, 32), (1, 8)))
    value_in = bell_draw(seeds[2], (L, D), 1.0, 6.0, ((0, 32), (1, 8)))
    cotangent = draw_cotangent(jax.random.fold_in(seeds[6], 71), 0)
    short_weight = bell_draw(seeds[4], (3, KS, D), 0.5, 3.0, ((2, 8),), jnp.float32)
    long_filter = draw_long_filter(jax.random.fold_in(seeds[6], 71), 0)
    return {"query_in": query_in, "key_in": key_in, "value_in": value_in, "cotangent": cotangent, "short_weight": short_weight, "long_filter": long_filter}


def phase_grid(left_index, right_index, period):
    product = left_index[:, None] * right_index[None, :] % period
    phases = 2.0 * math.pi / period * product.astype(jnp.float32)
    return (jnp.cos(phases), jnp.sin(phases))

def short_filter(extended, weights, local_rows):
    tap_count = weights.shape[0]
    result = jnp.zeros((local_rows, extended.shape[1]), jnp.float32)
    for lag_index in range(tap_count):
        offset_row = tap_count - 1 - lag_index
        result = result + weights[lag_index] * extended[offset_row:offset_row + local_rows].astype(jnp.float32)
    return result

def filter_back(extended, weights, local_rows):
    tap_count = weights.shape[0]
    result = jnp.zeros((local_rows, extended.shape[1]), jnp.float32)
    for lag_index in range(tap_count):
        result = result + weights[lag_index] * extended[lag_index:lag_index + local_rows].astype(jnp.float32)
    return result

def weight_terms(grads, extended, tap_count, local_rows):
    grad_float = grads.astype(jnp.float32)
    terms = []
    for lag_index in range(tap_count):
        offset_row = tap_count - 1 - lag_index
        terms.append(lax.optimization_barrier(jnp.sum(grad_float * extended[offset_row:offset_row + local_rows].astype(jnp.float32), axis=0)))
    return jnp.stack(terms)

def reference(query_in, key_in, value_in, cotangent, short_weight, long_filter):
    length = L
    fft_size = 2 * L
    inner_len = S
    outer_len = fft_size // inner_len
    half_rows = outer_len // 2
    rim_rows = KS - 1
    outer_ids = jnp.arange(outer_len, dtype=jnp.int32)
    half_ids = jnp.arange(half_rows, dtype=jnp.int32)
    inner_ids = jnp.arange(inner_len, dtype=jnp.int32)
    cos_first, sin_first = phase_grid(outer_ids, half_ids, outer_len)
    cos_first = cos_first.astype(jnp.bfloat16).astype(jnp.float32)
    sin_first = sin_first.astype(jnp.bfloat16).astype(jnp.float32)
    cos_inner, sin_inner = phase_grid(inner_ids, inner_ids, inner_len)
    cos_inner = cos_inner.astype(jnp.bfloat16).astype(jnp.float32)
    sin_inner = sin_inner.astype(jnp.bfloat16).astype(jnp.float32)
    turn_cos, turn_sin = phase_grid(outer_ids, inner_ids, fft_size)
    turn_cos = turn_cos[:, :, None]
    turn_sin = turn_sin[:, :, None]
    chan_block = min(D, 256)
    block_count = D // chan_block
    inv_root = 1.0 / math.sqrt(length)

    def split_rows(values_in):
        return values_in.reshape(length, block_count, chan_block).transpose(1, 0, 2)

    def forward_transform(signal):
        grid_rows = signal.reshape(half_rows, inner_len, chan_block).astype(jnp.float32)
        first_re = jnp.einsum('kr,rsc->ksc', cos_first, grid_rows)
        first_im = -jnp.einsum('kr,rsc->ksc', sin_first, grid_rows)
        twist_re = (first_re * turn_cos + first_im * turn_sin).astype(jnp.bfloat16).astype(jnp.float32)
        twist_im = (first_im * turn_cos - first_re * turn_sin).astype(jnp.bfloat16).astype(jnp.float32)
        spec_re = jnp.einsum('js,ksc->kjc', cos_inner, twist_re) + jnp.einsum('js,ksc->kjc', sin_inner, twist_im)
        spec_im = jnp.einsum('js,ksc->kjc', cos_inner, twist_im) - jnp.einsum('js,ksc->kjc', sin_inner, twist_re)
        return (spec_re.astype(jnp.bfloat16), spec_im.astype(jnp.bfloat16))

    def inverse_transform(spec_re, spec_im):
        spec_re = spec_re.astype(jnp.float32)
        spec_im = spec_im.astype(jnp.float32)
        back_re = jnp.einsum('sj,kjc->ksc', cos_inner, spec_re) - jnp.einsum('sj,kjc->ksc', sin_inner, spec_im)
        back_im = jnp.einsum('sj,kjc->ksc', cos_inner, spec_im) + jnp.einsum('sj,kjc->ksc', sin_inner, spec_re)
        untw_re = (back_re * turn_cos - back_im * turn_sin).astype(jnp.bfloat16).astype(jnp.float32)
        untw_im = (back_im * turn_cos + back_re * turn_sin).astype(jnp.bfloat16).astype(jnp.float32)
        signal = jnp.einsum('kr,ksc->rsc', cos_first, untw_re) - jnp.einsum('kr,ksc->rsc', sin_first, untw_im)
        signal = (signal * (1.0 / fft_size)).astype(jnp.bfloat16)
        return signal.reshape(length, chan_block)

    def spectral_product(spec_re, spec_im, filt_re, filt_im):
        spec_re = spec_re.astype(jnp.float32)
        spec_im = spec_im.astype(jnp.float32)
        prod_re = spec_re * filt_re - spec_im * filt_im
        prod_im = spec_re * filt_im + spec_im * filt_re
        return (prod_re.astype(jnp.bfloat16), prod_im.astype(jnp.bfloat16))

    def one_block(inputs):
        query_blk, key_blk, value_blk, cot_blk, weights, filter_blk = inputs
        pad_rows = jnp.zeros((rim_rows, chan_block), jnp.bfloat16)
        ext_query = jnp.concatenate([pad_rows, query_blk], axis=0)
        ext_key = jnp.concatenate([pad_rows, key_blk], axis=0)
        ext_value = jnp.concatenate([pad_rows, value_blk], axis=0)
        q_short = short_filter(ext_query, weights[0], length)
        k_short = short_filter(ext_key, weights[1], length)
        v_short = short_filter(ext_value, weights[2], length)
        mixed = (k_short * v_short).astype(jnp.bfloat16)
        spec_h = forward_transform(filter_blk)
        h_re = spec_h[0].astype(jnp.float32)
        h_im = spec_h[1].astype(jnp.float32)
        spec_x = forward_transform(mixed)
        product = spectral_product(spec_x[0], spec_x[1], h_re, h_im)
        conv = inverse_transform(product[0], product[1]).astype(jnp.float32)
        block_out = (q_short * conv).astype(jnp.bfloat16)
        cot_float = cot_blk.astype(jnp.float32)
        gq_short = (cot_float * conv).astype(jnp.bfloat16)
        grad_conv = (cot_float * q_short).astype(jnp.bfloat16)
        spec_g = forward_transform(grad_conv)
        back_product = spectral_product(spec_g[0], spec_g[1], h_re, -h_im)
        grad_mixed = inverse_transform(back_product[0], back_product[1]).astype(jnp.float32)
        gk_short = (grad_mixed * v_short).astype(jnp.bfloat16)
        gv_short = (grad_mixed * k_short).astype(jnp.bfloat16)
        ext_gq = jnp.concatenate([gq_short, pad_rows], axis=0)
        ext_gk = jnp.concatenate([gk_short, pad_rows], axis=0)
        ext_gv = jnp.concatenate([gv_short, pad_rows], axis=0)
        grad_q = filter_back(ext_gq, weights[0], length).astype(jnp.bfloat16)
        grad_k = filter_back(ext_gk, weights[1], length).astype(jnp.bfloat16)
        grad_v = filter_back(ext_gv, weights[2], length).astype(jnp.bfloat16)
        short_part = jnp.stack([weight_terms(gq_short, ext_query, KS, length), weight_terms(gk_short, ext_key, KS, length), weight_terms(gv_short, ext_value, KS, length)])
        x_re = spec_x[0].astype(jnp.float32)
        x_im = spec_x[1].astype(jnp.float32)
        g_re = spec_g[0].astype(jnp.float32)
        g_im = spec_g[1].astype(jnp.float32)
        cross_re = ((g_re * x_re + g_im * x_im) * inv_root).astype(jnp.bfloat16)
        cross_im = ((g_im * x_re - g_re * x_im) * inv_root).astype(jnp.bfloat16)
        grad_filt = inverse_transform(cross_re, cross_im)
        grad_short_blk = short_part * inv_root
        return (block_out, grad_q, grad_k, grad_v, grad_short_blk, grad_filt)
    weight_blocks = short_weight.reshape(3, KS, block_count, chan_block).transpose(2, 0, 1, 3)
    results = lax.map(one_block, (split_rows(query_in), split_rows(key_in), split_rows(value_in), split_rows(cotangent), weight_blocks, split_rows(long_filter)))

    def join_rows(values_in):
        return values_in.transpose(1, 0, 2).reshape(length, D)
    grad_short = results[4].transpose(1, 2, 0, 3).reshape(3, KS, D)
    return (join_rows(results[0]), join_rows(results[1]), join_rows(results[2]), join_rows(results[3]), grad_short, join_rows(results[5]))
```

```python
import functools
import math

import jax
import jax.numpy as jnp
from jax import lax
from jax.experimental import pallas as pl
from jax.experimental.pallas import tpu as pltpu
from jax.sharding import PartitionSpec as P

BF = jnp.bfloat16
F32 = jnp.float32
LANES = 128
VMEM_LIMIT = 48 * 1024 * 1024


def angles(left, right, period):
    product = left[:, None] * right[None, :] % (4 * period)
    return (2.0 * math.pi / (4 * period)) * product.astype(F32)


def filter_taps(scratch, at, weights, base):
    rows = scratch.shape[0] - 8
    total = weights[base : base + 1, :] * scratch[pl.ds(at, rows), :]
    for lag in range(1, 3):
        total = total + weights[base + lag : base + lag + 1, :] * scratch[pl.ds(at - lag, rows), :]
    return total


def stage(scratch, ref, halo, first):
    scratch[pl.ds(0, 8), :] = jnp.zeros((8, scratch.shape[1]), F32)
    scratch[pl.ds(6, 2), :] = halo[first : first + 2, :]
    scratch[pl.ds(8, ref.shape[0]), :] = ref[...].astype(F32)


def put_transposed(signal, out_ref, slot):
    for b in range(signal.shape[0] // LANES):
        turned = jnp.transpose(signal[b * LANES : (b + 1) * LANES, :]).astype(BF)
        out_ref[:, slot, b] = turned.reshape(out_ref.shape[0], out_ref.shape[3], LANES)


def pack_filter_kernel(h_ref, out_ref):
    put_transposed(h_ref[...].astype(F32), out_ref, 0)


def pack_signals_kernel(q_ref, k_ref, v_ref, cot_ref, halo_ref, w_ref, buf_ref, out_ref, qs, ks, vs):
    del buf_ref
    halo = halo_ref[...]
    w = w_ref[...]
    stage(qs, q_ref, halo, 0)
    stage(ks, k_ref, halo, 2)
    stage(vs, v_ref, halo, 4)
    q_short = filter_taps(qs, 8, w, 0)
    k_short = filter_taps(ks, 8, w, 3)
    v_short = filter_taps(vs, 8, w, 6)
    put_transposed(k_short * v_short, out_ref, 0)
    put_transposed(cot_ref[...].astype(F32) * q_short, out_ref, 1)


def spectral_kernel(
    inv_root, scale, group, in_ref, a_ref, b_ref, w_ref, wi_ref, c_ref, s_ref, out1, out2, xin, xout
):
    sources, arrays, halves, chans, _ = in_ref.shape
    rows = sources * halves
    for a in range(arrays):
        xin[a] = in_ref[:, a].reshape(rows * chans, LANES).astype(F32)
    cos_t = c_ref[...]
    sin_t = s_ref[...]
    n1 = cos_t.shape[0]

    def step(g, carry):
        spectra = []
        for a in range(arrays):
            cols = jnp.concatenate(
                [
                    xin[a, pl.ds(g * group + i, rows, stride=chans), :].astype(BF)
                    for i in range(group)
                ],
                axis=1,
            )
            first = jnp.dot(a_ref[...], cols, preferred_element_type=F32)
            parts = []
            for i in range(group):
                y_re = first[:n1, i * LANES : (i + 1) * LANES]
                y_im = first[n1:, i * LANES : (i + 1) * LANES]
                z_re = y_re * cos_t + y_im * sin_t
                z_im = y_im * cos_t - y_re * sin_t
                parts.append(jnp.concatenate([z_re.astype(BF), z_im.astype(BF)], axis=1))
            spectra.append(
                jnp.dot(jnp.concatenate(parts, axis=0), w_ref[...], preferred_element_type=F32)
            )
        (x_re, x_im), (g_re, g_im), (h_re, h_im) = [
            (f[:, :LANES], f[:, LANES:]) for f in spectra
        ]
        products = (
            (x_re * h_re - x_im * h_im, x_re * h_im + x_im * h_re),
            (g_re * h_re + g_im * h_im, g_im * h_re - g_re * h_im),
            ((g_re * x_re + g_im * x_im) * inv_root, (g_im * x_re - g_re * x_im) * inv_root),
        )
        for a, (p_re, p_im) in enumerate(products):
            spec = jnp.concatenate([p_re.astype(BF), p_im.astype(BF)], axis=1)
            back = jnp.dot(spec, wi_ref[...], preferred_element_type=F32)
            parts = []
            for i in range(group):
                u_re = back[i * n1 : (i + 1) * n1, :LANES]
                u_im = back[i * n1 : (i + 1) * n1, LANES:]
                v_re = u_re * cos_t - u_im * sin_t
                v_im = u_im * cos_t + u_re * sin_t
                parts.append(jnp.concatenate([v_re.astype(BF), v_im.astype(BF)], axis=0))
            signal = jnp.dot(
                b_ref[...], jnp.concatenate(parts, axis=1), preferred_element_type=F32
            )
            signal = signal * scale
            for i in range(group):
                xout[a, pl.ds(g * group + i, rows, stride=chans), :] = signal[
                    :, i * LANES : (i + 1) * LANES
                ]
        return carry

    lax.fori_loop(0, chans // group, step, 0)
    for a in range(2):
        out1[:, a] = xout[a].astype(BF).reshape(sources, halves, chans, LANES)
    out2[...] = xout[2].astype(BF).reshape(sources, halves, chans, LANES)


def get_transposed(in_ref, slot):
    blocks = []
    for b in range(in_ref.shape[2]):
        tile = in_ref[:, slot, b].reshape(LANES, LANES).astype(F32)
        blocks.append(jnp.transpose(tile))
    return jnp.concatenate(blocks, axis=0)


def finish_kernel(
    q_ref,
    k_ref,
    v_ref,
    cot_ref,
    halo_ref,
    w_ref,
    in_ref,
    out_ref,
    gq_ref,
    gk_ref,
    gv_ref,
    sums_ref,
    edge_ref,
    qs,
    ks,
    vs,
    gs,
):
    halo = halo_ref[...]
    w = w_ref[...]
    rows = q_ref.shape[0]
    stage(qs, q_ref, halo, 0)
    stage(ks, k_ref, halo, 2)
    stage(vs, v_ref, halo, 4)
    sums_ref[...] = jnp.zeros(sums_ref.shape, F32)
    edge_ref[...] = jnp.zeros(edge_ref.shape, F32)

    def finish(index, grad, staged, out):
        grad = grad.astype(BF).astype(F32)
        edge_ref[4 * index : 4 * index + 2, :] = grad[:2]
        edge_ref[4 * index + 2 : 4 * index + 4, :] = grad[rows - 2 :]
        gs[pl.ds(0, rows), :] = grad
        gs[pl.ds(rows, 8), :] = jnp.zeros((8, LANES), F32)
        back = w[3 * index : 3 * index + 1, :] * grad
        for lag in range(1, 3):
            back = back + w[3 * index + lag : 3 * index + lag + 1, :] * gs[pl.ds(lag, rows), :]
        out[...] = back.astype(BF)
        for lag in range(3):
            sums_ref[3 * index + lag : 3 * index + lag + 1, :] = jnp.sum(
                grad * staged[pl.ds(8 - lag, rows), :], axis=0, keepdims=True
            )

    conv = get_transposed(in_ref, 0)
    out_ref[...] = (filter_taps(qs, 8, w, 0) * conv).astype(BF)
    finish(0, cot_ref[...].astype(F32) * conv, qs, gq_ref)
    grad_mixed = get_transposed(in_ref, 1)
    finish(1, grad_mixed * filter_taps(vs, 8, w, 6), ks, gk_ref)
    finish(2, grad_mixed * filter_taps(ks, 8, w, 3), vs, gv_ref)


def unpack_kernel(in_ref, out_ref):
    for b in range(in_ref.shape[1]):
        tile = in_ref[:, b].reshape(LANES, LANES).astype(F32)
        out_ref[b * LANES : (b + 1) * LANES, :] = jnp.transpose(tile).astype(BF)


def params(**more):
    return pltpu.CompilerParams(vmem_limit_bytes=VMEM_LIMIT, **more)


def on_device(query_in, key_in, value_in, cotangent, short_weight, long_filter):
    rows, channels = query_in.shape
    taps = short_weight.shape[1]
    rim = taps - 1
    ctx = lax.axis_size("ctx")
    length = rows * ctx
    inv_root = 1.0 / math.sqrt(length)
    own = channels // ctx
    halves = rows // LANES
    outer = length // LANES
    tiles = channels // LANES
    per_tile = LANES // own
    w9 = short_weight.reshape(3 * taps, channels)

    r = jnp.arange(outer, dtype=jnp.int32)
    k1 = 4 * jnp.arange(outer, dtype=jnp.int32) + 1
    s = jnp.arange(LANES, dtype=jnp.int32)
    theta = angles(r, k1, outer).T
    a_mat = jnp.concatenate([jnp.cos(theta), -jnp.sin(theta)], axis=0).astype(BF)
    b_mat = a_mat.T
    phi = angles(s, k1, length).T
    cos_t, sin_t = jnp.cos(phi), jnp.sin(phi)
    psi = angles(s, 4 * s, LANES)
    c2, s2 = jnp.cos(psi), jnp.sin(psi)
    w_mat = jnp.concatenate(
        [jnp.concatenate([c2, -s2], axis=1), jnp.concatenate([s2, c2], axis=1)], axis=0
    ).astype(BF)
    wi_mat = w_mat.T

    up = [(i, i + 1) for i in range(ctx - 1)]
    down = [(i + 1, i) for i in range(ctx - 1)]
    tails = jnp.concatenate([x[rows - rim :] for x in (query_in, key_in, value_in)], axis=0)
    halo = lax.ppermute(tails, "ctx", up)
    halo = jnp.pad(halo.astype(F32), ((0, 8 - 3 * rim), (0, 0)))

    block = lambda: pl.BlockSpec((rows, LANES), lambda j: (0, j))
    row_block = lambda n: pl.BlockSpec((n, LANES), lambda j: (0, j))
    buf_shape = jax.ShapeDtypeStruct((ctx, 3, halves, own, LANES), BF)
    packed = pl.pallas_call(
        pack_filter_kernel,
        grid=(tiles,),
        in_specs=[block()],
        out_specs=pl.BlockSpec((per_tile, 1, halves, own, LANES), lambda j: (j, 2, 0, 0, 0)),
        out_shape=buf_shape,
        compiler_params=params(),
        name="pack_filter",
    )(long_filter)
    packed = pl.pallas_call(
        pack_signals_kernel,
        grid=(tiles,),
        in_specs=[block()] * 4
        + [row_block(8), row_block(9), pl.BlockSpec(memory_space=pl.ANY)],
        out_specs=pl.BlockSpec((per_tile, 2, halves, own, LANES), lambda j: (j, 0, 0, 0, 0)),
        out_shape=buf_shape,
        scratch_shapes=[pltpu.VMEM((rows + 8, LANES), F32)] * 3,
        input_output_aliases={6: 0},
        compiler_params=params(),
        name="pack_signals",
    )(query_in, key_in, value_in, cotangent, halo, w9, packed)
    arrived = lax.all_to_all(packed, "ctx", split_axis=0, concat_axis=0, tiled=True)

    cblock = 16
    whole = lambda x: pl.BlockSpec(x.shape, lambda i: (0,) * x.ndim)
    consts = (a_mat, b_mat, w_mat, wi_mat, cos_t, sin_t)
    out1, out2 = pl.pallas_call(
        functools.partial(spectral_kernel, inv_root, 1.0 / length, 4),
        grid=(own // cblock,),
        in_specs=[pl.BlockSpec((ctx, 3, halves, cblock, LANES), lambda i: (0, 0, 0, i, 0))]
        + [whole(x) for x in consts],
        out_specs=[
            pl.BlockSpec((ctx, 2, halves, cblock, LANES), lambda i: (0, 0, 0, i, 0)),
            pl.BlockSpec((ctx, halves, cblock, LANES), lambda i: (0, 0, i, 0)),
        ],
        out_shape=[
            jax.ShapeDtypeStruct((ctx, 2, halves, own, LANES), BF),
            jax.ShapeDtypeStruct((ctx, halves, own, LANES), BF),
        ],
        scratch_shapes=[pltpu.VMEM((3, outer * cblock, LANES), F32)] * 2,
        compiler_params=params(),
        name="spectral",
    )(arrived, *consts)
    back1 = lax.all_to_all(out1, "ctx", split_axis=0, concat_axis=0, tiled=True)
    back2 = lax.all_to_all(out2, "ctx", split_axis=0, concat_axis=0, tiled=True)

    wide = jax.ShapeDtypeStruct((rows, channels), BF)
    block_out, grad_q, grad_k, grad_v, sums, edge = pl.pallas_call(
        finish_kernel,
        grid=(tiles,),
        in_specs=[block()] * 4
        + [
            row_block(8),
            row_block(9),
            pl.BlockSpec((per_tile, 2, halves, own, LANES), lambda j: (j, 0, 0, 0, 0)),
        ],
        out_specs=[block()] * 4 + [row_block(16), row_block(16)],
        out_shape=[wide] * 4 + [jax.ShapeDtypeStruct((16, channels), F32)] * 2,
        scratch_shapes=[pltpu.VMEM((rows + 8, LANES), F32)] * 4,
        compiler_params=params(),
        name="finish",
    )(query_in, key_in, value_in, cotangent, halo, w9, back1)

    edge = edge[:12].reshape(3, 4, channels)
    ahead = lax.ppermute(edge[:, :2].astype(BF), "ctx", down).astype(F32)
    last = edge[:, 2:]
    w3 = short_weight
    row0 = w3[:, 0] * last[:, 0] + w3[:, 1] * last[:, 1] + w3[:, 2] * ahead[:, 0]
    row1 = w3[:, 0] * last[:, 1] + w3[:, 1] * ahead[:, 0] + w3[:, 2] * ahead[:, 1]
    fixed = jnp.stack([row0, row1], axis=1).astype(BF)
    grad_q = grad_q.at[rows - rim :].set(fixed[0])
    grad_k = grad_k.at[rows - rim :].set(fixed[1])
    grad_v = grad_v.at[rows - rim :].set(fixed[2])

    terms = sums[:9].reshape(9, ctx, own).transpose(1, 0, 2).reshape(ctx, 9 * own)
    terms = lax.all_to_all(terms, "ctx", split_axis=0, concat_axis=0, tiled=True)
    total = jnp.sum(terms, axis=0, keepdims=True)
    total = lax.all_to_all(
        jnp.broadcast_to(total, (ctx, 9 * own)), "ctx", split_axis=0, concat_axis=0, tiled=True
    )
    grad_short = total.reshape(ctx, 9, own).transpose(1, 0, 2).reshape(3, taps, channels) * inv_root

    grad_filter = pl.pallas_call(
        unpack_kernel,
        grid=(tiles,),
        in_specs=[pl.BlockSpec((per_tile, halves, own, LANES), lambda j: (j, 0, 0, 0))],
        out_specs=block(),
        out_shape=wide,
        compiler_params=params(),
        name="unpack_filter",
    )(back2)
    return (block_out, grad_q, grad_k, grad_v, grad_short, grad_filter)


def solution(mesh):
    wide = P("ctx", "tp")
    taps = P(None, None, "tp")
    return jax.shard_map(
        on_device,
        mesh=mesh,
        in_specs=(wide, wide, wide, wide, taps, wide),
        out_specs=(wide, wide, wide, wide, taps, wide),
        check_vma=False,
    )
```

```python
import functools
import math

import jax
import jax.numpy as jnp
from jax import lax
from jax.experimental import pallas as pl
from jax.experimental.pallas import tpu as pltpu
from jax.sharding import PartitionSpec as P
import numpy as np

BF = jnp.bfloat16
F32 = jnp.float32
LANES = 128
VMEM_LIMIT = 48 * 1024 * 1024
OUTS = (2, 1)


def tables(outer, length):
    r = np.arange(outer)
    k1 = 4 * np.arange(outer) + 1
    s = np.arange(LANES)
    theta = (k1[:, None] * r[None, :] % (4 * outer)) * (2.0 * math.pi / (4 * outer))
    phi = (k1[:, None] * s[None, :] % (4 * length)) * (2.0 * math.pi / (4 * length))
    psi = (s[:, None] * s[None, :] % LANES) * (2.0 * math.pi / LANES)
    first = np.concatenate([np.cos(theta), -np.sin(theta)], axis=0)
    c2, s2 = np.cos(psi), np.sin(psi)
    second = np.block([[c2, -s2], [s2, c2]])
    last = first.T / length
    as_bf = lambda x: jnp.asarray(x.astype(np.float32), BF)
    turn = np.stack([np.cos(phi), np.sin(phi)]).astype(np.float32)
    return as_bf(first), as_bf(last), as_bf(second), as_bf(second.T), jnp.asarray(turn)


def lane_tiles(ref):
    return [slice(t * LANES, (t + 1) * LANES) for t in range(ref.shape[-1] // LANES)]


def filter_taps(scratch, at, rows, weights, stream):
    total = weights[stream, 0:1, :] * scratch[pl.ds(at, rows), :]
    for lag in range(1, 3):
        total = total + weights[stream, lag : lag + 1, :] * scratch[pl.ds(at - lag, rows), :]
    return total


def stage(scratch, signal, halo):
    scratch[pl.ds(6, 2), :] = halo
    scratch[pl.ds(8, signal.shape[0]), :] = signal.astype(F32)


def put_transposed(signal, out_ref, tile, slot):
    own = out_ref.shape[3]
    per = LANES // own
    for b in range(signal.shape[0] // LANES):
        turned = jnp.transpose(signal[b * LANES : (b + 1) * LANES, :]).astype(BF)
        out_ref[tile * per : (tile + 1) * per, slot, b] = turned.reshape(per, own, LANES)


def get_transposed(in_ref, tile, slot):
    per = LANES // in_ref.shape[3]
    blocks = []
    for b in range(in_ref.shape[2]):
        part = in_ref[tile * per : (tile + 1) * per, slot, b].reshape(LANES, LANES)
        blocks.append(jnp.transpose(part.astype(F32)))
    return jnp.concatenate(blocks, axis=0)


def tails_kernel(q_ref, k_ref, v_ref, out_ref):
    rows = [ref[...].astype(F32)[14:, :] for ref in (q_ref, k_ref, v_ref)]
    fill = jnp.zeros((10, out_ref.shape[1]), F32)
    out_ref[...] = jnp.concatenate(rows + [fill], axis=0).astype(BF)


def pack_filter_kernel(h_ref, out_ref):
    for t, at in enumerate(lane_tiles(h_ref)):
        put_transposed(h_ref[:, at].astype(F32), out_ref, t, 0)


def pack_signals_kernel(q_ref, k_ref, v_ref, cot_ref, halo_ref, w_ref, buf_ref, out_ref, qs, ks, vs):
    del buf_ref
    rows = q_ref.shape[0]
    for t, at in enumerate(lane_tiles(q_ref)):
        halo = halo_ref[:, at].astype(F32)
        w = w_ref[:, :, at]
        stage(qs, q_ref[:, at], halo[0:2])
        stage(ks, k_ref[:, at], halo[2:4])
        stage(vs, v_ref[:, at], halo[4:6])
        mixed = filter_taps(ks, 8, rows, w, 1) * filter_taps(vs, 8, rows, w, 2)
        put_transposed(mixed, out_ref, t, 0)
        grad_conv = cot_ref[:, at].astype(F32) * filter_taps(qs, 8, rows, w, 0)
        put_transposed(grad_conv, out_ref, t, 1)


def spectral_kernel(inv_root, in_ref, a_ref, b_ref, w_ref, wi_ref, turn_ref, *rest):
    outs, (xin, xout) = rest[:-2], rest[-2:]
    sources, arrays, halves, chans, _ = in_ref.shape
    rows = sources * halves
    for a in range(arrays):
        xin[a] = in_ref[:, a].reshape(rows * chans, LANES).astype(F32)
    cos_t = turn_ref[0]
    sin_t = turn_ref[1]
    n1 = cos_t.shape[0]
    tiles = [slice(i * LANES, (i + 1) * LANES) for i in range(chans)]

    spectra = []
    for a in range(arrays):
        cols = jnp.concatenate(
            [xin[a, pl.ds(i, rows, stride=chans), :].astype(BF) for i in range(chans)], axis=1
        )
        first = jnp.dot(a_ref[...], cols, preferred_element_type=F32)
        parts = []
        for at in tiles:
            y_re = first[:n1, at]
            y_im = first[n1:, at]
            z_re = y_re * cos_t + y_im * sin_t
            z_im = y_im * cos_t - y_re * sin_t
            parts.append(jnp.concatenate([z_re.astype(BF), z_im.astype(BF)], axis=1))
        spectra.append(
            jnp.dot(jnp.concatenate(parts, axis=0), w_ref[...], preferred_element_type=F32)
        )
    (x_re, x_im), (g_re, g_im), (h_re, h_im) = [(f[:, :LANES], f[:, LANES:]) for f in spectra]
    products = (
        (x_re * h_re - x_im * h_im, x_re * h_im + x_im * h_re),
        (g_re * h_re + g_im * h_im, g_im * h_re - g_re * h_im),
        ((g_re * x_re + g_im * x_im) * inv_root, (g_im * x_re - g_re * x_im) * inv_root),
    )
    for a, (p_re, p_im) in enumerate(products):
        spec = jnp.concatenate([p_re.astype(BF), p_im.astype(BF)], axis=1)
        back = jnp.dot(spec, wi_ref[...], preferred_element_type=F32)
        parts = []
        for i in range(chans):
            u_re = back[i * n1 : (i + 1) * n1, :LANES]
            u_im = back[i * n1 : (i + 1) * n1, LANES:]
            v_re = u_re * cos_t - u_im * sin_t
            v_im = u_im * cos_t + u_re * sin_t
            parts.append(jnp.concatenate([v_re.astype(BF), v_im.astype(BF)], axis=0))
        signal = jnp.dot(b_ref[...], jnp.concatenate(parts, axis=1), preferred_element_type=F32)
        for i, at in enumerate(tiles):
            xout[a, pl.ds(i, rows, stride=chans), :] = signal[:, at]
    slots = [(out, j) for out in outs for j in range(out.shape[1])]
    for a, (out, j) in enumerate(slots):
        out[:, j] = xout[a].astype(BF).reshape(sources, halves, chans, LANES)


def finish_kernel(
    q_ref,
    k_ref,
    v_ref,
    cot_ref,
    halo_ref,
    w_ref,
    in_ref,
    out_ref,
    gq_ref,
    gk_ref,
    gv_ref,
    sums_ref,
    last_ref,
    qs,
    ks,
    vs,
    gs,
):
    rows = q_ref.shape[0]
    gs[pl.ds(rows, 8), :] = jnp.zeros((8, LANES), F32)
    for t, at in enumerate(lane_tiles(q_ref)):
        halo = halo_ref[:, at].astype(F32)
        w = w_ref[:, :, at]
        stage(qs, q_ref[:, at], halo[0:2])
        stage(ks, k_ref[:, at], halo[2:4])
        stage(vs, v_ref[:, at], halo[4:6])
        sums = []
        firsts = []
        lasts = []

        def finish(index, grad, staged, out):
            grad = grad.astype(BF).astype(F32)
            firsts.append(grad[:2])
            gs[pl.ds(0, rows), :] = grad
            back = w[index, 0:1, :] * grad
            for lag in range(1, 3):
                back = back + w[index, lag : lag + 1, :] * gs[pl.ds(lag, rows), :]
            out[:, at] = back.astype(BF)
            lasts.append(back[rows - 2 :])
            for lag in range(3):
                sums.append(
                    jnp.sum(grad * staged[pl.ds(8 - lag, rows), :], axis=0, keepdims=True)
                )

        conv = get_transposed(in_ref, t, 0)
        out_ref[:, at] = (filter_taps(qs, 8, rows, w, 0) * conv).astype(BF)
        finish(0, cot_ref[:, at].astype(F32) * conv, qs, gq_ref)
        grad_mixed = get_transposed(in_ref, t, 1)
        finish(1, grad_mixed * filter_taps(vs, 8, rows, w, 2), ks, gk_ref)
        finish(2, grad_mixed * filter_taps(ks, 8, rows, w, 1), vs, gv_ref)
        fill = [jnp.zeros((1, LANES), F32)]
        sums_ref[:, at] = jnp.concatenate(sums + fill + firsts, axis=0).astype(BF)
        last_ref[:, at] = jnp.concatenate(lasts + 2 * fill, axis=0)


def rim_kernel(ahead_ref, last_ref, w_ref, gq_in, gk_in, gv_in, gq_out, gk_out, gv_out):
    row = lax.broadcasted_iota(jnp.int32, (16, ahead_ref.shape[1]), 0)
    ahead = ahead_ref[...].astype(F32)
    streams = ((gq_in, gq_out), (gk_in, gk_out), (gv_in, gv_out))
    for i, (before, after) in enumerate(streams):
        w1 = w_ref[i, 1:2, :]
        w2 = w_ref[i, 2:3, :]
        next0 = ahead[10 + 2 * i : 11 + 2 * i]
        next1 = ahead[11 + 2 * i : 12 + 2 * i]
        end0 = last_ref[2 * i : 2 * i + 1] + w2 * next0
        end1 = last_ref[2 * i + 1 : 2 * i + 2] + w1 * next0 + w2 * next1
        fixed = jnp.where(row == 14, end0, jnp.where(row == 15, end1, before[...].astype(F32)))
        after[...] = fixed.astype(BF)


def unpack_kernel(slot, in_ref, out_ref):
    for t, at in enumerate(lane_tiles(out_ref)):
        out_ref[:, at] = get_transposed(in_ref, t, slot).astype(BF)


def sum_over_ctx(terms):
    ctx = lax.axis_size("ctx")

    def moved(x, to):
        return lax.ppermute(x.astype(BF), "ctx", [(i, to(i)) for i in range(ctx)]).astype(F32)

    total = terms.astype(F32)
    near = [moved(total, lambda i, d=d: i ^ d) for d in (1, 2, 3)]
    total = lax.reduce_precision((total + near[0]) + (near[1] + near[2]), 8, 7)
    far = [moved(total, lambda i, d=d: (i + d) % ctx) for d in (ctx // 4, ctx // 2, 3 * ctx // 4)]
    total = lax.reduce_precision((total + far[1]) + (far[0] + far[2]), 8, 7)
    for d in (ctx // 8,):
        total = total + moved(total, lambda i: i ^ d)
    return total


def params(**more):
    return pltpu.CompilerParams(vmem_limit_bytes=VMEM_LIMIT, **more)


def on_device(query_in, key_in, value_in, cotangent, short_weight, long_filter):
    rows, channels = query_in.shape
    taps = short_weight.shape[1]
    ctx = lax.axis_size("ctx")
    length = rows * ctx
    inv_root = 1.0 / math.sqrt(length)
    own = channels // ctx
    halves = rows // LANES
    outer = length // LANES
    wide_step = 512
    steps = channels // wide_step
    per_step = wide_step // own
    consts = tables(outer, length)

    up = [(i, i + 1) for i in range(ctx - 1)]
    down = [(i + 1, i) for i in range(ctx - 1)]
    block = lambda: pl.BlockSpec((rows, wide_step), lambda j: (0, j))
    row_block = lambda n: pl.BlockSpec((n, wide_step), lambda j: (0, j))
    w_block = lambda: pl.BlockSpec((3, taps, wide_step), lambda j: (0, 0, j))
    end_block = lambda: pl.BlockSpec((16, channels), lambda j: (rows // 16 - 1, 0))
    small = lambda n: pl.BlockSpec((n, channels), lambda j: (0, 0))

    tails = pl.pallas_call(
        tails_kernel,
        grid=(1,),
        in_specs=[end_block()] * 3,
        out_specs=small(16),
        out_shape=jax.ShapeDtypeStruct((16, channels), BF),
        name="tails",
    )(query_in, key_in, value_in)
    halo = lax.ppermute(tails, "ctx", up)

    buf_shape = jax.ShapeDtypeStruct((ctx, 3, halves, own, LANES), BF)
    packed = pl.pallas_call(
        pack_filter_kernel,
        grid=(steps,),
        in_specs=[block()],
        out_specs=pl.BlockSpec((per_step, 1, halves, own, LANES), lambda j: (j, 2, 0, 0, 0)),
        out_shape=buf_shape,
        compiler_params=params(),
        name="pack_filter",
    )(long_filter)
    packed = pl.pallas_call(
        pack_signals_kernel,
        grid=(steps,),
        in_specs=[block()] * 4 + [row_block(16), w_block(), pl.BlockSpec(memory_space=pl.ANY)],
        out_specs=pl.BlockSpec((per_step, 2, halves, own, LANES), lambda j: (j, 0, 0, 0, 0)),
        out_shape=buf_shape,
        scratch_shapes=[pltpu.VMEM((rows + 8, LANES), F32)] * 3,
        input_output_aliases={6: 0},
        compiler_params=params(),
        name="pack_signals",
    )(query_in, key_in, value_in, cotangent, halo, short_weight, packed)
    arrived = lax.all_to_all(packed, "ctx", split_axis=0, concat_axis=0, tiled=True)

    cblock = 16
    whole = lambda x: pl.BlockSpec(x.shape, lambda i: (0,) * x.ndim)
    outs = OUTS
    back = pl.pallas_call(
        functools.partial(spectral_kernel, inv_root),
        grid=(own // cblock,),
        in_specs=[pl.BlockSpec((ctx, 3, halves, cblock, LANES), lambda i: (0, 0, 0, i, 0))]
        + [whole(x) for x in consts],
        out_specs=[
            pl.BlockSpec((ctx, n, halves, cblock, LANES), lambda i: (0, 0, 0, i, 0)) for n in outs
        ],
        out_shape=[jax.ShapeDtypeStruct((ctx, n, halves, own, LANES), BF) for n in outs],
        scratch_shapes=[pltpu.VMEM((3, outer * cblock, LANES), F32)] * 2,
        compiler_params=params(),
        name="spectral",
    )(arrived, *consts)
    back = [lax.all_to_all(x, "ctx", split_axis=0, concat_axis=0, tiled=True) for x in back]

    wide = jax.ShapeDtypeStruct((rows, channels), BF)
    message = lambda n, at: pl.BlockSpec(
        (per_step, n, halves, own, LANES), lambda j: (j, at, 0, 0, 0)
    )
    block_out, grad_q, grad_k, grad_v, sums, last = pl.pallas_call(
        finish_kernel,
        grid=(steps,),
        in_specs=[block()] * 4 + [row_block(16), w_block(), message(2, 0)],
        out_specs=[block()] * 4 + [row_block(16), row_block(8)],
        out_shape=[wide] * 4
        + [
            jax.ShapeDtypeStruct((16, channels), BF),
            jax.ShapeDtypeStruct((8, channels), F32),
        ],
        scratch_shapes=[pltpu.VMEM((rows + 8, LANES), F32)] * 4,
        compiler_params=params(),
        name="finish",
    )(query_in, key_in, value_in, cotangent, halo, short_weight, back[0])

    ahead = lax.ppermute(sums, "ctx", down)
    grad_q, grad_k, grad_v = pl.pallas_call(
        rim_kernel,
        grid=(1,),
        in_specs=[small(16), small(8), pl.BlockSpec((3, taps, channels), lambda j: (0, 0, 0))]
        + [end_block()] * 3,
        out_specs=[end_block()] * 3,
        out_shape=[wide] * 3,
        input_output_aliases={3: 0, 4: 1, 5: 2},
        compiler_params=params(),
        name="rims",
    )(ahead, last, short_weight, grad_q, grad_k, grad_v)

    total = sum_over_ctx(sums)
    grad_short = total[: 3 * taps].reshape(3, taps, channels) * inv_root

    slot = 2 if len(outs) == 1 else 0
    grad_filter = pl.pallas_call(
        functools.partial(unpack_kernel, 0),
        grid=(steps,),
        in_specs=[message(1, slot)],
        out_specs=block(),
        out_shape=wide,
        compiler_params=params(),
        name="unpack_filter",
    )(back[-1])
    return (block_out, grad_q, grad_k, grad_v, grad_short, grad_filter)


def solution(mesh):
    wide = P("ctx", "tp")
    taps = P(None, None, "tp")
    return jax.shard_map(
        on_device,
        mesh=mesh,
        in_specs=(wide, wide, wide, wide, taps, wide),
        out_specs=(wide, wide, wide, wide, taps, wide),
        check_vma=False,
    )
```

```python
import functools
import math

import jax
import jax.numpy as jnp
from jax import lax
from jax.experimental import pallas as pl
from jax.experimental.pallas import tpu as pltpu
from jax.sharding import PartitionSpec as P
import numpy as np

BF = jnp.bfloat16
F32 = jnp.float32
LANES = 128


def tables(outer, length):
    r = np.arange(outer)
    k1 = 4 * np.arange(outer) + 1
    s = np.arange(LANES)
    theta = (k1[:, None] * r[None, :] % (4 * outer)) * (2.0 * math.pi / (4 * outer))
    phi = (k1[:, None] * s[None, :] % (4 * length)) * (2.0 * math.pi / (4 * length))
    psi = (s[:, None] * s[None, :] % LANES) * (2.0 * math.pi / LANES)
    first = np.concatenate([np.cos(theta), -np.sin(theta)], axis=0)
    c2, s2 = np.cos(psi), np.sin(psi)
    second = np.block([[c2, -s2], [s2, c2]])
    last = first.T / length
    as_bf = lambda x: jnp.asarray(x.astype(np.float32), BF)
    turn = np.stack([np.cos(phi), np.sin(phi)]).astype(np.float32)
    return as_bf(first), as_bf(last), as_bf(second), as_bf(second.T), jnp.asarray(turn)


def lane_tiles(ref):
    return [slice(t * LANES, (t + 1) * LANES) for t in range(ref.shape[-1] // LANES)]


def filter_taps(scratch, at, rows, weights, stream):
    total = weights[stream, 0:1, :] * scratch[pl.ds(at, rows), :]
    for lag in range(1, 3):
        total = total + weights[stream, lag : lag + 1, :] * scratch[pl.ds(at - lag, rows), :]
    return total


def stage(scratch, signal, halo):
    scratch[pl.ds(6, 2), :] = halo
    scratch[pl.ds(8, signal.shape[0]), :] = signal.astype(F32)


def put_transposed(signal, out_ref, tile, slot):
    own = out_ref.shape[3]
    per = LANES // own
    for b in range(signal.shape[0] // LANES):
        turned = jnp.transpose(signal[b * LANES : (b + 1) * LANES, :]).astype(BF)
        out_ref[tile * per : (tile + 1) * per, slot, b] = turned.reshape(per, own, LANES)


def get_transposed(in_ref, tile, slot):
    per = LANES // in_ref.shape[3]
    blocks = []
    for b in range(in_ref.shape[2]):
        part = in_ref[tile * per : (tile + 1) * per, slot, b].reshape(LANES, LANES)
        blocks.append(jnp.transpose(part.astype(F32)))
    return jnp.concatenate(blocks, axis=0)


def tails_kernel(q_ref, k_ref, v_ref, out_ref):
    rows = [ref[...].astype(F32)[14:, :] for ref in (q_ref, k_ref, v_ref)]
    fill = jnp.zeros((10, out_ref.shape[1]), F32)
    out_ref[...] = jnp.concatenate(rows + [fill], axis=0).astype(BF)


def pack_filter_kernel(h_ref, out_ref):
    for t, at in enumerate(lane_tiles(h_ref)):
        put_transposed(h_ref[:, at].astype(F32), out_ref, t, 2)


def pack_signals_kernel(q_ref, k_ref, v_ref, cot_ref, halo_ref, w_ref, buf_ref, out_ref, qs, ks, vs):
    del buf_ref
    rows = q_ref.shape[0]
    for t, at in enumerate(lane_tiles(q_ref)):
        halo = halo_ref[:, at].astype(F32)
        w = w_ref[:, :, at]
        stage(qs, q_ref[:, at], halo[0:2])
        stage(ks, k_ref[:, at], halo[2:4])
        stage(vs, v_ref[:, at], halo[4:6])
        mixed = filter_taps(ks, 8, rows, w, 1) * filter_taps(vs, 8, rows, w, 2)
        put_transposed(mixed, out_ref, t, 0)
        grad_conv = cot_ref[:, at].astype(F32) * filter_taps(qs, 8, rows, w, 0)
        put_transposed(grad_conv, out_ref, t, 1)


def to_spectrum(signal, a_ref, w_ref, turn_ref):
    sources, halves, chans, _ = signal.shape
    n1 = turn_ref.shape[1]
    cos_t, sin_t = turn_ref[0], turn_ref[1]
    by_chan = jnp.swapaxes(signal.reshape(sources * halves, chans, LANES).astype(F32), 0, 1)
    by_chan = by_chan.astype(BF)
    cols = jnp.concatenate([by_chan[i] for i in range(chans)], axis=1)
    first = jnp.dot(a_ref[...], cols, preferred_element_type=F32)
    parts = []
    for i in range(chans):
        y_re = first[:n1, i * LANES : (i + 1) * LANES]
        y_im = first[n1:, i * LANES : (i + 1) * LANES]
        z_re = y_re * cos_t + y_im * sin_t
        z_im = y_im * cos_t - y_re * sin_t
        parts.append(jnp.concatenate([z_re.astype(BF), z_im.astype(BF)], axis=1))
    spec = jnp.dot(jnp.concatenate(parts, axis=0), w_ref[...], preferred_element_type=F32)
    return spec[:, :LANES], spec[:, LANES:]


def from_spectrum(spec, chans, b_ref, wi_ref, turn_ref):
    n1 = turn_ref.shape[1]
    cos_t, sin_t = turn_ref[0], turn_ref[1]
    back = jnp.dot(spec, wi_ref[...], preferred_element_type=F32)
    parts = []
    for i in range(chans):
        u_re = back[i * n1 : (i + 1) * n1, :LANES]
        u_im = back[i * n1 : (i + 1) * n1, LANES:]
        v_re = u_re * cos_t - u_im * sin_t
        v_im = u_im * cos_t + u_re * sin_t
        parts.append(jnp.concatenate([v_re.astype(BF), v_im.astype(BF)], axis=0))
    signal = jnp.dot(b_ref[...], jnp.concatenate(parts, axis=1), preferred_element_type=F32)
    stacked = jnp.stack([signal[:, i * LANES : (i + 1) * LANES] for i in range(chans)], axis=0)
    return jnp.swapaxes(stacked, 0, 1).astype(BF)


def spectral_kernel(
    inv_root, in_ref, a_ref, b_ref, w_ref, wi_ref, turn_ref, streams_ref, filters_ref
):
    sources, _, halves, own, _ = in_ref.shape
    chans = 16
    for first in range(0, own, chans):
        at = slice(first, first + chans)

        def put(out_ref, slot, re, im):
            spec = jnp.concatenate([re.astype(BF), im.astype(BF)], axis=1)
            signal = from_spectrum(spec, chans, b_ref, wi_ref, turn_ref)
            out_ref[:, slot, :, at] = signal.reshape(sources, halves, chans, LANES)

        x_re, x_im = to_spectrum(in_ref[:, 0, :, at], a_ref, w_ref, turn_ref)
        h_re, h_im = to_spectrum(in_ref[:, 2, :, at], a_ref, w_ref, turn_ref)
        put(streams_ref, 0, x_re * h_re - x_im * h_im, x_re * h_im + x_im * h_re)
        g_re, g_im = to_spectrum(in_ref[:, 1, :, at], a_ref, w_ref, turn_ref)
        put(streams_ref, 1, g_re * h_re + g_im * h_im, g_im * h_re - g_re * h_im)
        cross_re = (g_re * x_re + g_im * x_im) * inv_root
        cross_im = (g_im * x_re - g_re * x_im) * inv_root
        put(filters_ref, 0, cross_re, cross_im)


def local_terms(refs, halo_ref, w_ref, in_ref, scratch, t, at):
    q_ref, k_ref, v_ref, cot_ref = refs
    rows = q_ref.shape[0]
    halo = halo_ref[:, at].astype(F32)
    w = w_ref[:, :, at]
    for i, ref in enumerate((q_ref, k_ref, v_ref)):
        stage(scratch[i], ref[:, at], halo[2 * i : 2 * i + 2])
    conv = get_transposed(in_ref, t, 0)
    grad_mixed = get_transposed(in_ref, t, 1)
    grads = (
        cot_ref[:, at].astype(F32) * conv,
        grad_mixed * filter_taps(scratch[2], 8, rows, w, 2),
        grad_mixed * filter_taps(scratch[1], 8, rows, w, 1),
    )
    return w, conv, [grad.astype(BF).astype(F32) for grad in grads]


def sums_kernel(
    q_ref, k_ref, v_ref, cot_ref, halo_ref, w_ref, in_ref, sums_ref, qs, ks, vs
):
    refs = (q_ref, k_ref, v_ref, cot_ref)
    rows = q_ref.shape[0]
    for t, at in enumerate(lane_tiles(q_ref)):
        _, _, grads = local_terms(refs, halo_ref, w_ref, in_ref, (qs, ks, vs), t, at)
        out = []
        for grad, staged in zip(grads, (qs, ks, vs)):
            for lag in range(3):
                out.append(jnp.sum(grad * staged[pl.ds(8 - lag, rows), :], axis=0, keepdims=True))
        out.append(jnp.zeros((1, LANES), F32))
        out.extend(grad[:2] for grad in grads)
        sums_ref[:, at] = jnp.concatenate(out, axis=0).astype(BF)


def finish_kernel(
    q_ref,
    k_ref,
    v_ref,
    cot_ref,
    halo_ref,
    w_ref,
    in_ref,
    out_ref,
    gq_ref,
    gk_ref,
    gv_ref,
    last_ref,
    qs,
    ks,
    vs,
    gs,
):
    refs = (q_ref, k_ref, v_ref, cot_ref)
    rows = q_ref.shape[0]
    gs[pl.ds(rows, 8), :] = jnp.zeros((8, LANES), F32)
    for t, at in enumerate(lane_tiles(q_ref)):
        w, conv, grads = local_terms(refs, halo_ref, w_ref, in_ref, (qs, ks, vs), t, at)
        out_ref[:, at] = (filter_taps(qs, 8, rows, w, 0) * conv).astype(BF)
        lasts = []
        for i, (grad, out) in enumerate(zip(grads, (gq_ref, gk_ref, gv_ref))):
            gs[pl.ds(0, rows), :] = grad
            back = w[i, 0:1, :] * grad
            for lag in range(1, 3):
                back = back + w[i, lag : lag + 1, :] * gs[pl.ds(lag, rows), :]
            out[:, at] = back.astype(BF)
            lasts.append(back[rows - 2 :])
        lasts.append(jnp.zeros((2, LANES), F32))
        last_ref[:, at] = jnp.concatenate(lasts, axis=0)


def unpack_kernel(in_ref, out_ref):
    for t, at in enumerate(lane_tiles(out_ref)):
        out_ref[:, at] = get_transposed(in_ref, t, 0).astype(BF)


def close_kernel(
    inv_root,
    mine_ref,
    other_ref,
    near_ref,
    last_ref,
    w_ref,
    gq_in,
    gk_in,
    gv_in,
    short_ref,
    gq_out,
    gk_out,
    gv_out,
):
    mine = mine_ref[...]
    other = other_ref[...].astype(F32)
    total = (mine + other) * inv_root
    ahead = jnp.where(mine > 0.0, other, near_ref[...])
    row = lax.broadcasted_iota(jnp.int32, mine.shape, 0)
    streams = ((gq_in, gq_out), (gk_in, gk_out), (gv_in, gv_out))
    for i, (before, after) in enumerate(streams):
        short_ref[i] = total[3 * i : 3 * i + 3]
        w1 = w_ref[i, 1:2, :]
        w2 = w_ref[i, 2:3, :]
        next0 = ahead[10 + 2 * i : 11 + 2 * i]
        next1 = ahead[11 + 2 * i : 12 + 2 * i]
        end0 = last_ref[2 * i : 2 * i + 1] + w2 * next0
        end1 = last_ref[2 * i + 1 : 2 * i + 2] + w1 * next0 + w2 * next1
        fixed = jnp.where(row == 14, end0, jnp.where(row == 15, end1, before[...].astype(F32)))
        after[...] = fixed.astype(BF)


def sum_over_ctx(terms, beside):
    ctx = lax.axis_size("ctx")
    rank = lax.axis_index("ctx")
    slow, fast = rank // 4, rank % 4
    summed = lax.broadcasted_iota(jnp.int32, terms.shape, 0) < 10

    def moved(x, to):
        return lax.ppermute(x.astype(BF), "ctx", [(i, to(i)) for i in range(ctx)]).astype(F32)

    mine = terms.astype(F32)
    near = [moved(mine, lambda i, d=d: i ^ d) for d in (1, 2, 3)]
    total = lax.reduce_precision((mine + near[0]) + (near[1] + near[2]), 8, 7)
    heads = mine
    for d in (1, 2, 3):
        heads = jnp.where(fast == d, near[d - 1], heads)
    beyond = jnp.where(fast == 1, near[2], near[0])
    beyond = jnp.where(fast == 3, 0.0, beyond)
    total = jnp.where(summed, total, heads)
    total, beyond, beside = lax.optimization_barrier((total, beyond, beside))
    far = [moved(total, lambda i, d=d: (i + d) % ctx) for d in (ctx // 4, ctx // 2, 3 * ctx // 4)]
    heads = jnp.where(slow % 2 == 0, far[2], total)
    total = lax.reduce_precision((total + far[1]) + (far[0] + far[2]), 8, 7)
    other = lax.ppermute(
        jnp.where(summed, total, heads).astype(BF), "ctx", [(i, i ^ (ctx // 8)) for i in range(ctx)]
    )
    takes = jnp.where((fast == 3) & (rank < ctx - 1), 1.0, 0.0)
    return jnp.where(summed, total, takes), other, beyond, beside


def params(mib=32):
    return pltpu.CompilerParams(vmem_limit_bytes=mib * 1024 * 1024)


def on_device(query_in, key_in, value_in, cotangent, short_weight, long_filter):
    rows, channels = query_in.shape
    taps = short_weight.shape[1]
    ctx = lax.axis_size("ctx")
    length = rows * ctx
    inv_root = 1.0 / math.sqrt(length)
    own = channels // ctx
    halves = rows // LANES
    outer = length // LANES
    wide_step = 512
    steps = channels // wide_step
    per_step = wide_step // own
    consts = tables(outer, length)

    up = [(i, i + 1) for i in range(ctx - 1)]
    block = lambda: pl.BlockSpec((rows, wide_step), lambda j: (0, j))
    row_block = lambda n: pl.BlockSpec((n, wide_step), lambda j: (0, j))
    w_block = lambda: pl.BlockSpec((3, taps, wide_step), lambda j: (0, 0, j))
    end_block = lambda: pl.BlockSpec((16, channels), lambda j: (rows // 16 - 1, 0))
    small = lambda n: pl.BlockSpec((n, channels), lambda j: (0, 0))

    tails = pl.pallas_call(
        tails_kernel,
        grid=(1,),
        in_specs=[end_block()] * 3,
        out_specs=small(16),
        out_shape=jax.ShapeDtypeStruct((16, channels), BF),
        name="tails",
    )(query_in, key_in, value_in)
    halo = lax.ppermute(tails, "ctx", up)

    buf_shape = jax.ShapeDtypeStruct((ctx, 3, halves, own, LANES), BF)
    in_vmem = pl.BlockSpec(memory_space=pltpu.VMEM)
    packed = pl.pallas_call(
        pack_filter_kernel,
        in_specs=[in_vmem],
        out_specs=in_vmem,
        out_shape=buf_shape,
        compiler_params=params(),
        name="pack_filter",
    )(long_filter)
    packed = pl.pallas_call(
        pack_signals_kernel,
        in_specs=[in_vmem] * 7,
        out_specs=in_vmem,
        out_shape=buf_shape,
        scratch_shapes=[pltpu.VMEM((rows + 8, LANES), F32)] * 3,
        input_output_aliases={6: 0},
        compiler_params=params(),
        name="pack_signals",
    )(query_in, key_in, value_in, cotangent, halo, short_weight, packed)
    arrived = lax.all_to_all(packed, "ctx", split_axis=0, concat_axis=0, tiled=True)

    streams, filters = pl.pallas_call(
        functools.partial(spectral_kernel, inv_root),
        in_specs=[in_vmem] * (1 + len(consts)),
        out_specs=[in_vmem] * 2,
        out_shape=[jax.ShapeDtypeStruct((ctx, n, halves, own, LANES), BF) for n in (2, 1)],
        compiler_params=params(),
        name="spectral",
    )(arrived, *consts)
    streams = lax.all_to_all(streams, "ctx", split_axis=0, concat_axis=0, tiled=True)
    filters = lax.all_to_all(filters, "ctx", split_axis=0, concat_axis=0, tiled=True)

    wide = jax.ShapeDtypeStruct((rows, channels), BF)
    message = pl.BlockSpec((per_step, 2, halves, own, LANES), lambda j: (j, 0, 0, 0, 0))
    local_specs = [block()] * 4 + [row_block(16), w_block(), message]
    local_args = (query_in, key_in, value_in, cotangent, halo, short_weight, streams)
    sums = pl.pallas_call(
        sums_kernel,
        in_specs=[in_vmem] * len(local_args),
        out_specs=in_vmem,
        out_shape=jax.ShapeDtypeStruct((16, channels), BF),
        scratch_shapes=[pltpu.VMEM((rows + 8, LANES), F32)] * 3,
        compiler_params=params(),
        name="sums",
    )(*local_args)
    block_out, grad_q, grad_k, grad_v, last = pl.pallas_call(
        finish_kernel,
        grid=(steps,),
        in_specs=local_specs,
        out_specs=[block()] * 4 + [row_block(8)],
        out_shape=[wide] * 4 + [jax.ShapeDtypeStruct((8, channels), F32)],
        scratch_shapes=[pltpu.VMEM((rows + 8, LANES), F32)] * 4,
        compiler_params=params(),
        name="finish",
    )(*local_args)

    grad_filter = pl.pallas_call(
        unpack_kernel,
        grid=(steps,),
        in_specs=[pl.BlockSpec((per_step, 1, halves, own, LANES), lambda j: (j, 0, 0, 0, 0))],
        out_specs=block(),
        out_shape=wide,
        compiler_params=params(),
        name="unpack_filter",
    )(filters)

    mine, other, beyond, last = sum_over_ctx(sums, last)
    all_taps = lambda: pl.BlockSpec((3, taps, channels), lambda j: (0, 0, 0))
    grad_short, grad_q, grad_k, grad_v = pl.pallas_call(
        functools.partial(close_kernel, inv_root),
        grid=(1,),
        in_specs=[small(16)] * 3 + [small(8), all_taps()] + [end_block()] * 3,
        out_specs=[all_taps()] + [end_block()] * 3,
        out_shape=[jax.ShapeDtypeStruct((3, taps, channels), F32)] + [wide] * 3,
        input_output_aliases={5: 1, 6: 2, 7: 3},
        compiler_params=params(),
        name="close",
    )(mine, other, beyond, last, short_weight, grad_q, grad_k, grad_v)
    return (block_out, grad_q, grad_k, grad_v, grad_short, grad_filter)


def solution(mesh):
    wide = P("ctx", "tp")
    taps = P(None, None, "tp")
    return jax.shard_map(
        on_device,
        mesh=mesh,
        in_specs=(wide, wide, wide, wide, taps, wide),
        out_specs=(wide, wide, wide, wide, taps, wide),
        check_vma=False,
    )
```

```python
import functools
import math

import jax
import jax.numpy as jnp
from jax import lax
from jax.experimental import pallas as pl
from jax.experimental.pallas import tpu as pltpu
from jax.sharding import PartitionSpec as P
import numpy as np

BF = jnp.bfloat16
F32 = jnp.float32
LANES = 128


def tables(outer, length):
    r = np.arange(outer)
    k1 = 4 * np.arange(outer) + 1
    s = np.arange(LANES)
    theta = (k1[:, None] * r[None, :] % (4 * outer)) * (2.0 * math.pi / (4 * outer))
    phi = (k1[:, None] * s[None, :] % (4 * length)) * (2.0 * math.pi / (4 * length))
    psi = (s[:, None] * s[None, :] % LANES) * (2.0 * math.pi / LANES)
    first = np.concatenate([np.cos(theta), -np.sin(theta)], axis=0)
    c2, s2 = np.cos(psi), np.sin(psi)
    second = np.block([[c2, -s2], [s2, c2]])
    last = first.T / length
    as_bf = lambda x: jnp.asarray(x.astype(np.float32), BF)
    turn = np.stack([np.cos(phi), np.sin(phi)]).astype(np.float32)
    return as_bf(first), as_bf(last), as_bf(second), as_bf(second.T), jnp.asarray(turn)


def lane_tiles(ref):
    return [slice(t * LANES, (t + 1) * LANES) for t in range(ref.shape[-1] // LANES)]


def filter_taps(scratch, at, rows, weights, stream):
    total = weights[stream, 0:1, :] * scratch[pl.ds(at, rows), :]
    for lag in range(1, 3):
        total = total + weights[stream, lag : lag + 1, :] * scratch[pl.ds(at - lag, rows), :]
    return total


def stage(scratch, signal, halo):
    scratch[pl.ds(6, 2), :] = halo
    scratch[pl.ds(8, signal.shape[0]), :] = signal.astype(F32)


def put_transposed(signal, out_ref, tile, slot):
    own = out_ref.shape[3]
    per = LANES // own
    for b in range(signal.shape[0] // LANES):
        turned = jnp.transpose(signal[b * LANES : (b + 1) * LANES, :]).astype(BF)
        out_ref[tile * per : (tile + 1) * per, slot, b] = turned.reshape(per, own, LANES)


def get_transposed(in_ref, tile, slot):
    per = LANES // in_ref.shape[3]
    blocks = []
    for b in range(in_ref.shape[2]):
        part = in_ref[tile * per : (tile + 1) * per, slot, b].reshape(LANES, LANES)
        blocks.append(jnp.transpose(part.astype(F32)))
    return jnp.concatenate(blocks, axis=0)


def tails_kernel(q_ref, k_ref, v_ref, out_ref, buf, sems):
    refs = (q_ref, k_ref, v_ref)
    copies = [
        pltpu.make_async_copy(ref.at[pl.ds(ref.shape[0] - 16, 16), :], buf.at[i], sems.at[i])
        for i, ref in enumerate(refs)
    ]
    for copy in copies:
        copy.start()
    for copy in copies:
        copy.wait()
    rows = [buf[i].astype(F32)[14:, :] for i in range(3)]
    fill = jnp.zeros((10, out_ref.shape[1]), F32)
    out_ref[...] = jnp.concatenate(rows + [fill], axis=0).astype(BF)


def pack_filter_kernel(h_ref, out_ref):
    for t, at in enumerate(lane_tiles(h_ref)):
        put_transposed(h_ref[:, at].astype(F32), out_ref, t, 2)


def pack_signals_kernel(q_ref, k_ref, v_ref, cot_ref, halo_ref, w_ref, buf_ref, out_ref, qs, ks, vs):
    del buf_ref
    rows = q_ref.shape[0]
    for t, at in enumerate(lane_tiles(q_ref)):
        halo = halo_ref[:, at].astype(F32)
        w = w_ref[:, :, at]
        stage(qs, q_ref[:, at], halo[0:2])
        stage(ks, k_ref[:, at], halo[2:4])
        stage(vs, v_ref[:, at], halo[4:6])
        mixed = filter_taps(ks, 8, rows, w, 1) * filter_taps(vs, 8, rows, w, 2)
        put_transposed(mixed, out_ref, t, 0)
        grad_conv = cot_ref[:, at].astype(F32) * filter_taps(qs, 8, rows, w, 0)
        put_transposed(grad_conv, out_ref, t, 1)


def to_spectrum(signal, a_ref, w_ref, turn_ref):
    sources, halves, chans, _ = signal.shape
    n1 = turn_ref.shape[1]
    cos_t, sin_t = turn_ref[0], turn_ref[1]
    by_chan = jnp.swapaxes(signal.reshape(sources * halves, chans, LANES).astype(F32), 0, 1)
    by_chan = by_chan.astype(BF)
    cols = jnp.concatenate([by_chan[i] for i in range(chans)], axis=1)
    first = jnp.dot(a_ref[...], cols, preferred_element_type=F32)
    parts = []
    for i in range(chans):
        y_re = first[:n1, i * LANES : (i + 1) * LANES]
        y_im = first[n1:, i * LANES : (i + 1) * LANES]
        z_re = y_re * cos_t + y_im * sin_t
        z_im = y_im * cos_t - y_re * sin_t
        parts.append(jnp.concatenate([z_re.astype(BF), z_im.astype(BF)], axis=1))
    spec = jnp.dot(jnp.concatenate(parts, axis=0), w_ref[...], preferred_element_type=F32)
    return spec[:, :LANES], spec[:, LANES:]


def from_spectrum(spec, chans, b_ref, wi_ref, turn_ref):
    n1 = turn_ref.shape[1]
    cos_t, sin_t = turn_ref[0], turn_ref[1]
    back = jnp.dot(spec, wi_ref[...], preferred_element_type=F32)
    parts = []
    for i in range(chans):
        u_re = back[i * n1 : (i + 1) * n1, :LANES]
        u_im = back[i * n1 : (i + 1) * n1, LANES:]
        v_re = u_re * cos_t - u_im * sin_t
        v_im = u_im * cos_t + u_re * sin_t
        parts.append(jnp.concatenate([v_re.astype(BF), v_im.astype(BF)], axis=0))
    signal = jnp.dot(b_ref[...], jnp.concatenate(parts, axis=1), preferred_element_type=F32)
    stacked = jnp.stack([signal[:, i * LANES : (i + 1) * LANES] for i in range(chans)], axis=0)
    return jnp.swapaxes(stacked, 0, 1).astype(BF)


def spectral_kernel(
    inv_root, in_ref, a_ref, b_ref, w_ref, wi_ref, turn_ref, streams_ref, filters_ref
):
    sources, _, halves, own, _ = in_ref.shape
    chans = 32
    for first in range(0, own, chans):
        at = slice(first, first + chans)

        def put(out_ref, slot, re, im):
            spec = jnp.concatenate([re.astype(BF), im.astype(BF)], axis=1)
            signal = from_spectrum(spec, chans, b_ref, wi_ref, turn_ref)
            out_ref[:, slot, :, at] = signal.reshape(sources, halves, chans, LANES)

        x_re, x_im = to_spectrum(in_ref[:, 0, :, at], a_ref, w_ref, turn_ref)
        h_re, h_im = to_spectrum(in_ref[:, 2, :, at], a_ref, w_ref, turn_ref)
        put(streams_ref, 0, x_re * h_re - x_im * h_im, x_re * h_im + x_im * h_re)
        g_re, g_im = to_spectrum(in_ref[:, 1, :, at], a_ref, w_ref, turn_ref)
        put(streams_ref, 1, g_re * h_re + g_im * h_im, g_im * h_re - g_re * h_im)
        cross_re = (g_re * x_re + g_im * x_im) * inv_root
        cross_im = (g_im * x_re - g_re * x_im) * inv_root
        put(filters_ref, 0, cross_re, cross_im)


def local_terms(refs, halo_ref, w_ref, in_ref, scratch, t, at):
    q_ref, k_ref, v_ref, cot_ref = refs
    rows = q_ref.shape[0]
    halo = halo_ref[:, at].astype(F32)
    w = w_ref[:, :, at]
    for i, ref in enumerate((q_ref, k_ref, v_ref)):
        stage(scratch[i], ref[:, at], halo[2 * i : 2 * i + 2])
    conv = get_transposed(in_ref, t, 0)
    grad_mixed = get_transposed(in_ref, t, 1)
    grads = (
        cot_ref[:, at].astype(F32) * conv,
        grad_mixed * filter_taps(scratch[2], 8, rows, w, 2),
        grad_mixed * filter_taps(scratch[1], 8, rows, w, 1),
    )
    return w, conv, [grad.astype(BF).astype(F32) for grad in grads]


def sums_kernel(
    q_ref, k_ref, v_ref, cot_ref, halo_ref, w_ref, in_ref, sums_ref, qs, ks, vs
):
    refs = (q_ref, k_ref, v_ref, cot_ref)
    rows = q_ref.shape[0]
    for t, at in enumerate(lane_tiles(q_ref)):
        _, _, grads = local_terms(refs, halo_ref, w_ref, in_ref, (qs, ks, vs), t, at)
        out = []
        for grad, staged in zip(grads, (qs, ks, vs)):
            for lag in range(3):
                out.append(jnp.sum(grad * staged[pl.ds(8 - lag, rows), :], axis=0, keepdims=True))
        out.append(jnp.zeros((1, LANES), F32))
        out.extend(grad[:2] for grad in grads)
        sums_ref[:, at] = jnp.concatenate(out, axis=0).astype(BF)


def finish_kernel(
    q_ref,
    k_ref,
    v_ref,
    cot_ref,
    halo_ref,
    w_ref,
    in_ref,
    out_ref,
    gq_ref,
    gk_ref,
    gv_ref,
    last_ref,
    qs,
    ks,
    vs,
    gs,
):
    refs = (q_ref, k_ref, v_ref, cot_ref)
    rows = q_ref.shape[0]
    gs[pl.ds(rows, 8), :] = jnp.zeros((8, LANES), F32)
    for t, at in enumerate(lane_tiles(q_ref)):
        w, conv, grads = local_terms(refs, halo_ref, w_ref, in_ref, (qs, ks, vs), t, at)
        out_ref[:, at] = (filter_taps(qs, 8, rows, w, 0) * conv).astype(BF)
        for i, (grad, out) in enumerate(zip(grads, (gq_ref, gk_ref, gv_ref))):
            gs[pl.ds(0, rows), :] = grad
            back = w[i, 0:1, :] * grad
            for lag in range(1, 3):
                back = back + w[i, lag : lag + 1, :] * gs[pl.ds(lag, rows), :]
            out[:, at] = back.astype(BF)
            last_ref[i, :, at] = back[rows - 16 :]


def unpack_kernel(in_ref, out_ref):
    for t, at in enumerate(lane_tiles(out_ref)):
        out_ref[:, at] = get_transposed(in_ref, t, 0).astype(BF)


def close_kernel(
    inv_root,
    mine_ref,
    other_ref,
    near_ref,
    last_ref,
    w_ref,
    gq_in,
    gk_in,
    gv_in,
    short_ref,
    gq_out,
    gk_out,
    gv_out,
    short,
    ends,
    sems,
):
    del gq_in, gk_in, gv_in
    mine = mine_ref[...]
    other = other_ref[...].astype(F32)
    total = (mine + other) * inv_root
    ahead = jnp.where(mine > 0.0, other, near_ref[...])
    row = lax.broadcasted_iota(jnp.int32, mine.shape, 0)
    copies = []
    for i, out in enumerate((gq_out, gk_out, gv_out)):
        short[i] = total[3 * i : 3 * i + 3]
        w1 = w_ref[i, 1:2, :]
        w2 = w_ref[i, 2:3, :]
        next0 = ahead[10 + 2 * i : 11 + 2 * i]
        next1 = ahead[11 + 2 * i : 12 + 2 * i]
        last = last_ref[i]
        end1 = last + w1 * next0 + w2 * next1
        fixed = jnp.where(row == 14, last + w2 * next0, jnp.where(row == 15, end1, last))
        ends[i] = fixed.astype(BF)
        copies.append(
            pltpu.make_async_copy(
                ends.at[i], out.at[pl.ds(out.shape[0] - 16, 16), :], sems.at[i]
            )
        )
        copies[-1].start()
    copies.append(pltpu.make_async_copy(short, short_ref, sems.at[3]))
    copies[-1].start()
    for copy in copies:
        copy.wait()


def sum_over_ctx(terms, beside):
    ctx = lax.axis_size("ctx")
    rank = lax.axis_index("ctx")
    slow, fast = rank // 4, rank % 4
    summed = lax.broadcasted_iota(jnp.int32, terms.shape, 0) < 10

    def moved(x, to):
        return lax.ppermute(x.astype(BF), "ctx", [(i, to(i)) for i in range(ctx)]).astype(F32)

    mine = terms.astype(F32)
    near = [moved(mine, lambda i, d=d: i ^ d) for d in (1, 2, 3)]
    total = lax.reduce_precision((mine + near[0]) + (near[1] + near[2]), 8, 7)
    heads = mine
    for d in (1, 2, 3):
        heads = jnp.where(fast == d, near[d - 1], heads)
    beyond = jnp.where(fast == 1, near[2], near[0])
    beyond = jnp.where(fast == 3, 0.0, beyond)
    total = jnp.where(summed, total, heads)
    total, beyond, beside = lax.optimization_barrier((total, beyond, beside))
    far = [moved(total, lambda i, d=d: (i + d) % ctx) for d in (ctx // 4, ctx // 2, 3 * ctx // 4)]
    heads = jnp.where(slow % 2 == 0, far[2], total)
    total = lax.reduce_precision((total + far[1]) + (far[0] + far[2]), 8, 7)
    other = lax.ppermute(
        jnp.where(summed, total, heads).astype(BF), "ctx", [(i, i ^ (ctx // 8)) for i in range(ctx)]
    )
    takes = jnp.where((fast == 3) & (rank < ctx - 1), 1.0, 0.0)
    return jnp.where(summed, total, takes), other, beyond, beside


def params(mib=32):
    return pltpu.CompilerParams(vmem_limit_bytes=mib * 1024 * 1024)


def on_device(query_in, key_in, value_in, cotangent, short_weight, long_filter):
    rows, channels = query_in.shape
    taps = short_weight.shape[1]
    ctx = lax.axis_size("ctx")
    length = rows * ctx
    inv_root = 1.0 / math.sqrt(length)
    own = channels // ctx
    halves = rows // LANES
    outer = length // LANES
    wide_step = 512
    steps = channels // wide_step
    per_step = wide_step // own
    consts = tables(outer, length)

    up = [(i, i + 1) for i in range(ctx - 1)]
    block = lambda: pl.BlockSpec((rows, wide_step), lambda j: (0, j))
    row_block = lambda n: pl.BlockSpec((n, wide_step), lambda j: (0, j))
    w_block = lambda: pl.BlockSpec((3, taps, wide_step), lambda j: (0, 0, j))

    in_vmem = pl.BlockSpec(memory_space=pltpu.VMEM)
    anywhere = pl.BlockSpec(memory_space=pl.ANY)
    tails = pl.pallas_call(
        tails_kernel,
        in_specs=[anywhere] * 3,
        out_specs=in_vmem,
        out_shape=jax.ShapeDtypeStruct((16, channels), BF),
        scratch_shapes=[pltpu.VMEM((3, 16, channels), BF), pltpu.SemaphoreType.DMA((3,))],
        name="tails",
    )(query_in, key_in, value_in)
    halo = lax.ppermute(tails, "ctx", up)

    buf_shape = jax.ShapeDtypeStruct((ctx, 3, halves, own, LANES), BF)
    packed = pl.pallas_call(
        pack_filter_kernel,
        in_specs=[in_vmem],
        out_specs=in_vmem,
        out_shape=buf_shape,
        compiler_params=params(),
        name="pack_filter",
    )(long_filter)
    packed = pl.pallas_call(
        pack_signals_kernel,
        in_specs=[in_vmem] * 7,
        out_specs=in_vmem,
        out_shape=buf_shape,
        scratch_shapes=[pltpu.VMEM((rows + 8, LANES), F32)] * 3,
        input_output_aliases={6: 0},
        compiler_params=params(),
        name="pack_signals",
    )(query_in, key_in, value_in, cotangent, halo, short_weight, packed)
    arrived = lax.all_to_all(packed, "ctx", split_axis=0, concat_axis=0, tiled=True)

    streams, filters = pl.pallas_call(
        functools.partial(spectral_kernel, inv_root),
        in_specs=[in_vmem] * (1 + len(consts)),
        out_specs=[in_vmem] * 2,
        out_shape=[jax.ShapeDtypeStruct((ctx, n, halves, own, LANES), BF) for n in (2, 1)],
        compiler_params=params(),
        name="spectral",
    )(arrived, *consts)
    streams = lax.all_to_all(streams, "ctx", split_axis=0, concat_axis=0, tiled=True)
    filters = lax.all_to_all(filters, "ctx", split_axis=0, concat_axis=0, tiled=True)

    wide = jax.ShapeDtypeStruct((rows, channels), BF)
    message = pl.BlockSpec((per_step, 2, halves, own, LANES), lambda j: (j, 0, 0, 0, 0))
    local_specs = [block()] * 4 + [row_block(16), w_block(), message]
    local_args = (query_in, key_in, value_in, cotangent, halo, short_weight, streams)
    sums = pl.pallas_call(
        sums_kernel,
        in_specs=[in_vmem] * len(local_args),
        out_specs=in_vmem,
        out_shape=jax.ShapeDtypeStruct((16, channels), BF),
        scratch_shapes=[pltpu.VMEM((rows + 8, LANES), F32)] * 3,
        compiler_params=params(),
        name="sums",
    )(*local_args)
    block_out, grad_q, grad_k, grad_v, last = pl.pallas_call(
        finish_kernel,
        grid=(steps,),
        in_specs=local_specs,
        out_specs=[block()] * 4 + [pl.BlockSpec((3, 16, wide_step), lambda j: (0, 0, j))],
        out_shape=[wide] * 4 + [jax.ShapeDtypeStruct((3, 16, channels), F32)],
        scratch_shapes=[pltpu.VMEM((rows + 8, LANES), F32)] * 4,
        compiler_params=params(),
        name="finish",
    )(*local_args)

    grad_filter = pl.pallas_call(
        unpack_kernel,
        grid=(steps,),
        in_specs=[pl.BlockSpec((per_step, 1, halves, own, LANES), lambda j: (j, 0, 0, 0, 0))],
        out_specs=block(),
        out_shape=wide,
        compiler_params=params(),
        name="unpack_filter",
    )(filters)

    mine, other, beyond, last = sum_over_ctx(sums, last)
    grad_short, grad_q, grad_k, grad_v = pl.pallas_call(
        functools.partial(close_kernel, inv_root),
        in_specs=[in_vmem] * 5 + [anywhere] * 3,
        out_specs=[anywhere] * 4,
        out_shape=[jax.ShapeDtypeStruct((3, taps, channels), F32)] + [wide] * 3,
        scratch_shapes=[
            pltpu.VMEM((3, taps, channels), F32),
            pltpu.VMEM((3, 16, channels), BF),
            pltpu.SemaphoreType.DMA((4,)),
        ],
        input_output_aliases={5: 1, 6: 2, 7: 3},
        compiler_params=params(),
        name="close",
    )(mine, other, beyond, last, short_weight, grad_q, grad_k, grad_v)
    return (block_out, grad_q, grad_k, grad_v, grad_short, grad_filter)


def solution(mesh):
    wide = P("ctx", "tp")
    taps = P(None, None, "tp")
    return jax.shard_map(
        on_device,
        mesh=mesh,
        in_specs=(wide, wide, wide, wide, taps, wide),
        out_specs=(wide, wide, wide, wide, taps, wide),
        check_vma=False,
    )
```

```python
import functools
import math

import jax
import jax.numpy as jnp
from jax import lax
from jax.experimental import pallas as pl
from jax.experimental.pallas import tpu as pltpu
from jax.sharding import PartitionSpec as P
import numpy as np

BF = jnp.bfloat16
F32 = jnp.float32
LANES = 128


def tables(outer, length):
    r = np.arange(outer)
    k1 = 4 * np.arange(outer) + 1
    s = np.arange(LANES)
    theta = (k1[:, None] * r[None, :] % (4 * outer)) * (2.0 * math.pi / (4 * outer))
    phi = (k1[:, None] * s[None, :] % (4 * length)) * (2.0 * math.pi / (4 * length))
    psi = (s[:, None] * s[None, :] % LANES) * (2.0 * math.pi / LANES)
    first = np.concatenate([np.cos(theta), -np.sin(theta)], axis=0)
    c2, s2 = np.cos(psi), np.sin(psi)
    second = np.block([[c2, -s2], [s2, c2]])
    last = first.T / length
    as_bf = lambda x: jnp.asarray(x.astype(np.float32), BF)
    turn = np.stack([np.cos(phi), np.sin(phi)]).astype(np.float32)
    return as_bf(first), as_bf(last), as_bf(second), as_bf(second.T), jnp.asarray(turn)


def lane_tiles(ref):
    return [slice(t * LANES, (t + 1) * LANES) for t in range(ref.shape[-1] // LANES)]


def filter_taps(scratch, at, rows, weights, stream):
    total = weights[stream, 0:1, :] * scratch[pl.ds(at, rows), :]
    for lag in range(1, 3):
        total = total + weights[stream, lag : lag + 1, :] * scratch[pl.ds(at - lag, rows), :]
    return total


def stage(scratch, signal, halo):
    scratch[pl.ds(6, 2), :] = halo
    scratch[pl.ds(8, signal.shape[0]), :] = signal.astype(F32)


def put_transposed(signal, out_ref, tile, slot):
    own = out_ref.shape[3]
    per = LANES // own
    for b in range(signal.shape[0] // LANES):
        turned = jnp.transpose(signal[b * LANES : (b + 1) * LANES, :]).astype(BF)
        out_ref[tile * per : (tile + 1) * per, slot, b] = turned.reshape(per, own, LANES)


def get_transposed(in_ref, tile, slot):
    per = LANES // in_ref.shape[3]
    blocks = []
    for b in range(in_ref.shape[2]):
        part = in_ref[tile * per : (tile + 1) * per, slot, b].reshape(LANES, LANES)
        blocks.append(jnp.transpose(part.astype(F32)))
    return jnp.concatenate(blocks, axis=0)


def tails_kernel(q_ref, k_ref, v_ref, out_ref):
    rows = [ref[...].astype(F32)[14:, :] for ref in (q_ref, k_ref, v_ref)]
    fill = jnp.zeros((10, out_ref.shape[1]), F32)
    out_ref[...] = jnp.concatenate(rows + [fill], axis=0).astype(BF)


def pack_filter_kernel(h_ref, out_ref):
    for t, at in enumerate(lane_tiles(h_ref)):
        put_transposed(h_ref[:, at].astype(F32), out_ref, t, 2)


def pack_signals_kernel(q_ref, k_ref, v_ref, cot_ref, halo_ref, w_ref, buf_ref, out_ref, qs, ks, vs):
    del buf_ref
    rows = q_ref.shape[0]
    for t, at in enumerate(lane_tiles(q_ref)):
        halo = halo_ref[:, at].astype(F32)
        w = w_ref[:, :, at]
        stage(qs, q_ref[:, at], halo[0:2])
        stage(ks, k_ref[:, at], halo[2:4])
        stage(vs, v_ref[:, at], halo[4:6])
        mixed = filter_taps(ks, 8, rows, w, 1) * filter_taps(vs, 8, rows, w, 2)
        put_transposed(mixed, out_ref, t, 0)
        grad_conv = cot_ref[:, at].astype(F32) * filter_taps(qs, 8, rows, w, 0)
        put_transposed(grad_conv, out_ref, t, 1)


def to_spectrum(signal, a_ref, w_ref, turn_ref):
    sources, halves, chans, _ = signal.shape
    n1 = turn_ref.shape[1]
    cos_t, sin_t = turn_ref[0], turn_ref[1]
    by_chan = jnp.swapaxes(signal.reshape(sources * halves, chans, LANES).astype(F32), 0, 1)
    by_chan = by_chan.astype(BF)
    cols = jnp.concatenate([by_chan[i] for i in range(chans)], axis=1)
    first = jnp.dot(a_ref[...], cols, preferred_element_type=F32)
    parts = []
    for i in range(chans):
        y_re = first[:n1, i * LANES : (i + 1) * LANES]
        y_im = first[n1:, i * LANES : (i + 1) * LANES]
        z_re = y_re * cos_t + y_im * sin_t
        z_im = y_im * cos_t - y_re * sin_t
        parts.append(jnp.concatenate([z_re.astype(BF), z_im.astype(BF)], axis=1))
    spec = jnp.dot(jnp.concatenate(parts, axis=0), w_ref[...], preferred_element_type=F32)
    return spec[:, :LANES], spec[:, LANES:]


def from_spectrum(spec, chans, b_ref, wi_ref, turn_ref):
    n1 = turn_ref.shape[1]
    cos_t, sin_t = turn_ref[0], turn_ref[1]
    back = jnp.dot(spec, wi_ref[...], preferred_element_type=F32)
    parts = []
    for i in range(chans):
        u_re = back[i * n1 : (i + 1) * n1, :LANES]
        u_im = back[i * n1 : (i + 1) * n1, LANES:]
        v_re = u_re * cos_t - u_im * sin_t
        v_im = u_im * cos_t + u_re * sin_t
        parts.append(jnp.concatenate([v_re.astype(BF), v_im.astype(BF)], axis=0))
    signal = jnp.dot(b_ref[...], jnp.concatenate(parts, axis=1), preferred_element_type=F32)
    stacked = jnp.stack([signal[:, i * LANES : (i + 1) * LANES] for i in range(chans)], axis=0)
    return jnp.swapaxes(stacked, 0, 1).astype(BF)


def spectral_kernel(
    inv_root, in_ref, a_ref, b_ref, w_ref, wi_ref, turn_ref, streams_ref, filters_ref
):
    sources, _, halves, own, _ = in_ref.shape
    chans = 32
    for first in range(0, own, chans):
        at = slice(first, first + chans)

        def put(out_ref, slot, re, im):
            spec = jnp.concatenate([re.astype(BF), im.astype(BF)], axis=1)
            signal = from_spectrum(spec, chans, b_ref, wi_ref, turn_ref)
            out_ref[:, slot, :, at] = signal.reshape(sources, halves, chans, LANES)

        x_re, x_im = to_spectrum(in_ref[:, 0, :, at], a_ref, w_ref, turn_ref)
        h_re, h_im = to_spectrum(in_ref[:, 2, :, at], a_ref, w_ref, turn_ref)
        put(streams_ref, 0, x_re * h_re - x_im * h_im, x_re * h_im + x_im * h_re)
        g_re, g_im = to_spectrum(in_ref[:, 1, :, at], a_ref, w_ref, turn_ref)
        put(streams_ref, 1, g_re * h_re + g_im * h_im, g_im * h_re - g_re * h_im)
        cross_re = (g_re * x_re + g_im * x_im) * inv_root
        cross_im = (g_im * x_re - g_re * x_im) * inv_root
        put(filters_ref, 0, cross_re, cross_im)


def local_terms(refs, halo_ref, w_ref, in_ref, scratch, t, at):
    q_ref, k_ref, v_ref, cot_ref = refs
    rows = q_ref.shape[0]
    halo = halo_ref[:, at].astype(F32)
    w = w_ref[:, :, at]
    for i, ref in enumerate((q_ref, k_ref, v_ref)):
        stage(scratch[i], ref[:, at], halo[2 * i : 2 * i + 2])
    conv = get_transposed(in_ref, t, 0)
    grad_mixed = get_transposed(in_ref, t, 1)
    grads = (
        cot_ref[:, at].astype(F32) * conv,
        grad_mixed * filter_taps(scratch[2], 8, rows, w, 2),
        grad_mixed * filter_taps(scratch[1], 8, rows, w, 1),
    )
    return w, conv, [grad.astype(BF).astype(F32) for grad in grads]


def sums_kernel(
    q_ref, k_ref, v_ref, cot_ref, halo_ref, w_ref, in_ref, sums_ref, qs, ks, vs
):
    refs = (q_ref, k_ref, v_ref, cot_ref)
    rows = q_ref.shape[0]
    for t, at in enumerate(lane_tiles(q_ref)):
        _, _, grads = local_terms(refs, halo_ref, w_ref, in_ref, (qs, ks, vs), t, at)
        out = []
        for grad, staged in zip(grads, (qs, ks, vs)):
            for lag in range(3):
                out.append(jnp.sum(grad * staged[pl.ds(8 - lag, rows), :], axis=0, keepdims=True))
        out.append(jnp.zeros((1, LANES), F32))
        out.extend(grad[:2] for grad in grads)
        sums_ref[:, at] = jnp.concatenate(out, axis=0).astype(BF)


def finish_kernel(
    q_ref,
    k_ref,
    v_ref,
    cot_ref,
    halo_ref,
    w_ref,
    in_ref,
    out_ref,
    gq_ref,
    gk_ref,
    gv_ref,
    last_ref,
    qs,
    ks,
    vs,
    gs,
):
    refs = (q_ref, k_ref, v_ref, cot_ref)
    rows = q_ref.shape[0]
    gs[pl.ds(rows, 8), :] = jnp.zeros((8, LANES), F32)
    for t, at in enumerate(lane_tiles(q_ref)):
        w, conv, grads = local_terms(refs, halo_ref, w_ref, in_ref, (qs, ks, vs), t, at)
        out_ref[:, at] = (filter_taps(qs, 8, rows, w, 0) * conv).astype(BF)
        lasts = []
        for i, (grad, out) in enumerate(zip(grads, (gq_ref, gk_ref, gv_ref))):
            gs[pl.ds(0, rows), :] = grad
            back = w[i, 0:1, :] * grad
            for lag in range(1, 3):
                back = back + w[i, lag : lag + 1, :] * gs[pl.ds(lag, rows), :]
            out[:, at] = back.astype(BF)
            lasts.append(back[rows - 2 :])
        lasts.append(jnp.zeros((2, LANES), F32))
        last_ref[:, at] = jnp.concatenate(lasts, axis=0)


def unpack_kernel(in_ref, out_ref):
    for t, at in enumerate(lane_tiles(out_ref)):
        out_ref[:, at] = get_transposed(in_ref, t, 0).astype(BF)


def close_kernel(
    inv_root,
    mine_ref,
    other_ref,
    near_ref,
    last_ref,
    w_ref,
    gq_in,
    gk_in,
    gv_in,
    short_ref,
    gq_out,
    gk_out,
    gv_out,
):
    mine = mine_ref[...]
    other = other_ref[...].astype(F32)
    total = (mine + other) * inv_root
    ahead = jnp.where(mine > 0.0, other, near_ref[...])
    row = lax.broadcasted_iota(jnp.int32, mine.shape, 0)
    streams = ((gq_in, gq_out), (gk_in, gk_out), (gv_in, gv_out))
    for i, (before, after) in enumerate(streams):
        short_ref[i] = total[3 * i : 3 * i + 3]
        w1 = w_ref[i, 1:2, :]
        w2 = w_ref[i, 2:3, :]
        next0 = ahead[10 + 2 * i : 11 + 2 * i]
        next1 = ahead[11 + 2 * i : 12 + 2 * i]
        end0 = last_ref[2 * i : 2 * i + 1] + w2 * next0
        end1 = last_ref[2 * i + 1 : 2 * i + 2] + w1 * next0 + w2 * next1
        fixed = jnp.where(row == 14, end0, jnp.where(row == 15, end1, before[...].astype(F32)))
        after[...] = fixed.astype(BF)


def sum_over_ctx(terms, beside):
    ctx = lax.axis_size("ctx")
    rank = lax.axis_index("ctx")
    slow, fast = rank // 4, rank % 4
    summed = lax.broadcasted_iota(jnp.int32, terms.shape, 0) < 10

    def moved(x, to):
        return lax.ppermute(x.astype(BF), "ctx", [(i, to(i)) for i in range(ctx)]).astype(F32)

    mine = terms.astype(F32)
    near = [moved(mine, lambda i, d=d: i ^ d) for d in (1, 2, 3)]
    total = lax.reduce_precision((mine + near[0]) + (near[1] + near[2]), 8, 7)
    heads = mine
    for d in (1, 2, 3):
        heads = jnp.where(fast == d, near[d - 1], heads)
    beyond = jnp.where(fast == 1, near[2], near[0])
    beyond = jnp.where(fast == 3, 0.0, beyond)
    total = jnp.where(summed, total, heads)
    total, beyond, beside = lax.optimization_barrier((total, beyond, beside))
    far = [moved(total, lambda i, d=d: (i + d) % ctx) for d in (ctx // 4, ctx // 2, 3 * ctx // 4)]
    heads = jnp.where(slow % 2 == 0, far[2], total)
    total = lax.reduce_precision((total + far[1]) + (far[0] + far[2]), 8, 7)
    other = lax.ppermute(
        jnp.where(summed, total, heads).astype(BF), "ctx", [(i, i ^ (ctx // 8)) for i in range(ctx)]
    )
    takes = jnp.where((fast == 3) & (rank < ctx - 1), 1.0, 0.0)
    return jnp.where(summed, total, takes), other, beyond, beside


def params(mib=32):
    return pltpu.CompilerParams(vmem_limit_bytes=mib * 1024 * 1024)


def on_device(query_in, key_in, value_in, cotangent, short_weight, long_filter):
    rows, channels = query_in.shape
    taps = short_weight.shape[1]
    ctx = lax.axis_size("ctx")
    length = rows * ctx
    inv_root = 1.0 / math.sqrt(length)
    own = channels // ctx
    halves = rows // LANES
    outer = length // LANES
    wide_step = 512
    steps = channels // wide_step
    per_step = wide_step // own
    consts = tables(outer, length)

    up = [(i, i + 1) for i in range(ctx - 1)]
    block = lambda: pl.BlockSpec((rows, wide_step), lambda j: (0, j))
    row_block = lambda n: pl.BlockSpec((n, wide_step), lambda j: (0, j))
    w_block = lambda: pl.BlockSpec((3, taps, wide_step), lambda j: (0, 0, j))
    end_block = lambda: pl.BlockSpec((16, channels), lambda j: (rows // 16 - 1, 0))
    small = lambda n: pl.BlockSpec((n, channels), lambda j: (0, 0))

    tails = pl.pallas_call(
        tails_kernel,
        grid=(1,),
        in_specs=[end_block()] * 3,
        out_specs=small(16),
        out_shape=jax.ShapeDtypeStruct((16, channels), BF),
        name="tails",
    )(query_in, key_in, value_in)
    halo = lax.ppermute(tails, "ctx", up)

    buf_shape = jax.ShapeDtypeStruct((ctx, 3, halves, own, LANES), BF)
    in_vmem = pl.BlockSpec(memory_space=pltpu.VMEM)
    packed = pl.pallas_call(
        pack_filter_kernel,
        in_specs=[in_vmem],
        out_specs=in_vmem,
        out_shape=buf_shape,
        compiler_params=params(),
        name="pack_filter",
    )(long_filter)
    packed = pl.pallas_call(
        pack_signals_kernel,
        in_specs=[in_vmem] * 7,
        out_specs=in_vmem,
        out_shape=buf_shape,
        scratch_shapes=[pltpu.VMEM((rows + 8, LANES), F32)] * 3,
        input_output_aliases={6: 0},
        compiler_params=params(),
        name="pack_signals",
    )(query_in, key_in, value_in, cotangent, halo, short_weight, packed)
    arrived = lax.all_to_all(packed, "ctx", split_axis=0, concat_axis=0, tiled=True)

    streams, filters = pl.pallas_call(
        functools.partial(spectral_kernel, inv_root),
        in_specs=[in_vmem] * (1 + len(consts)),
        out_specs=[in_vmem] * 2,
        out_shape=[jax.ShapeDtypeStruct((ctx, n, halves, own, LANES), BF) for n in (2, 1)],
        compiler_params=params(),
        name="spectral",
    )(arrived, *consts)
    streams = lax.all_to_all(streams, "ctx", split_axis=0, concat_axis=0, tiled=True)
    filters = lax.all_to_all(filters, "ctx", split_axis=0, concat_axis=0, tiled=True)

    wide = jax.ShapeDtypeStruct((rows, channels), BF)
    message = pl.BlockSpec((per_step, 2, halves, own, LANES), lambda j: (j, 0, 0, 0, 0))
    local_specs = [block()] * 4 + [row_block(16), w_block(), message]
    local_args = (query_in, key_in, value_in, cotangent, halo, short_weight, streams)
    sums = pl.pallas_call(
        sums_kernel,
        in_specs=[in_vmem] * len(local_args),
        out_specs=in_vmem,
        out_shape=jax.ShapeDtypeStruct((16, channels), BF),
        scratch_shapes=[pltpu.VMEM((rows + 8, LANES), F32)] * 3,
        compiler_params=params(),
        name="sums",
    )(*local_args)
    block_out, grad_q, grad_k, grad_v, last = pl.pallas_call(
        finish_kernel,
        grid=(steps,),
        in_specs=local_specs,
        out_specs=[block()] * 4 + [row_block(8)],
        out_shape=[wide] * 4 + [jax.ShapeDtypeStruct((8, channels), F32)],
        scratch_shapes=[pltpu.VMEM((rows + 8, LANES), F32)] * 4,
        compiler_params=params(),
        name="finish",
    )(*local_args)

    grad_filter = pl.pallas_call(
        unpack_kernel,
        grid=(steps,),
        in_specs=[pl.BlockSpec((per_step, 1, halves, own, LANES), lambda j: (j, 0, 0, 0, 0))],
        out_specs=block(),
        out_shape=wide,
        compiler_params=params(),
        name="unpack_filter",
    )(filters)

    mine, other, beyond, last = sum_over_ctx(sums, last)
    all_taps = lambda: pl.BlockSpec((3, taps, channels), lambda j: (0, 0, 0))
    grad_short, grad_q, grad_k, grad_v = pl.pallas_call(
        functools.partial(close_kernel, inv_root),
        grid=(1,),
        in_specs=[small(16)] * 3 + [small(8), all_taps()] + [end_block()] * 3,
        out_specs=[all_taps()] + [end_block()] * 3,
        out_shape=[jax.ShapeDtypeStruct((3, taps, channels), F32)] + [wide] * 3,
        input_output_aliases={5: 1, 6: 2, 7: 3},
        compiler_params=params(),
        name="close",
    )(mine, other, beyond, last, short_weight, grad_q, grad_k, grad_v)
    return (block_out, grad_q, grad_k, grad_v, grad_short, grad_filter)


def solution(mesh):
    wide = P("ctx", "tp")
    taps = P(None, None, "tp")
    return jax.shard_map(
        on_device,
        mesh=mesh,
        in_specs=(wide, wide, wide, wide, taps, wide),
        out_specs=(wide, wide, wide, wide, taps, wide),
        check_vma=False,
    )
```

```python
import functools
import math

import jax
import jax.numpy as jnp
from jax import lax
from jax.experimental import pallas as pl
from jax.experimental.pallas import tpu as pltpu
from jax.sharding import PartitionSpec as P
import numpy as np

BF = jnp.bfloat16
F32 = jnp.float32
LANES = 128


def tables(outer, length):
    r = np.arange(outer)
    k1 = 4 * np.arange(outer) + 1
    s = np.arange(LANES)
    theta = (k1[:, None] * r[None, :] % (4 * outer)) * (2.0 * math.pi / (4 * outer))
    phi = (k1[:, None] * s[None, :] % (4 * length)) * (2.0 * math.pi / (4 * length))
    psi = (s[:, None] * s[None, :] % LANES) * (2.0 * math.pi / LANES)
    first = np.concatenate([np.cos(theta), -np.sin(theta)], axis=0)
    c2, s2 = np.cos(psi), np.sin(psi)
    second = np.block([[c2, -s2], [s2, c2]])
    last = first.T / length
    as_bf = lambda x: jnp.asarray(x.astype(np.float32), BF)
    turn = np.stack([np.cos(phi), np.sin(phi)]).astype(np.float32)
    return as_bf(first), as_bf(last), as_bf(second), as_bf(second.T), jnp.asarray(turn)


def lane_tiles(ref):
    return [slice(t * LANES, (t + 1) * LANES) for t in range(ref.shape[-1] // LANES)]


def filter_taps(scratch, at, rows, weights, stream):
    total = weights[stream, 0:1, :] * scratch[pl.ds(at, rows), :]
    for lag in range(1, 3):
        total = total + weights[stream, lag : lag + 1, :] * scratch[pl.ds(at - lag, rows), :]
    return total


def stage(scratch, signal, halo):
    scratch[pl.ds(6, 2), :] = halo
    scratch[pl.ds(8, signal.shape[0]), :] = signal.astype(F32)


def put_transposed(signal, out_ref, tile, slot):
    own = out_ref.shape[3]
    per = LANES // own
    for b in range(signal.shape[0] // LANES):
        turned = jnp.transpose(signal[b * LANES : (b + 1) * LANES, :]).astype(BF)
        out_ref[tile * per : (tile + 1) * per, slot, b] = turned.reshape(per, own, LANES)


def get_transposed(in_ref, tile, slot):
    per = LANES // in_ref.shape[3]
    blocks = []
    for b in range(in_ref.shape[2]):
        part = in_ref[tile * per : (tile + 1) * per, slot, b].reshape(LANES, LANES)
        blocks.append(jnp.transpose(part.astype(F32)))
    return jnp.concatenate(blocks, axis=0)


def tails_kernel(q_ref, k_ref, v_ref, out_ref):
    rows = [ref[...].astype(F32)[14:, :] for ref in (q_ref, k_ref, v_ref)]
    fill = jnp.zeros((10, out_ref.shape[1]), F32)
    out_ref[...] = jnp.concatenate(rows + [fill], axis=0).astype(BF)


def pack_filter_kernel(h_ref, out_ref):
    for t, at in enumerate(lane_tiles(h_ref)):
        put_transposed(h_ref[:, at].astype(F32), out_ref, t, 2)


def pack_signals_kernel(q_ref, k_ref, v_ref, cot_ref, halo_ref, w_ref, buf_ref, out_ref, qs, ks, vs):
    del buf_ref
    rows = q_ref.shape[0]
    for t, at in enumerate(lane_tiles(q_ref)):
        halo = halo_ref[:, at].astype(F32)
        w = w_ref[:, :, at]
        stage(qs, q_ref[:, at], halo[0:2])
        stage(ks, k_ref[:, at], halo[2:4])
        stage(vs, v_ref[:, at], halo[4:6])
        mixed = filter_taps(ks, 8, rows, w, 1) * filter_taps(vs, 8, rows, w, 2)
        put_transposed(mixed, out_ref, t, 0)
        grad_conv = cot_ref[:, at].astype(F32) * filter_taps(qs, 8, rows, w, 0)
        put_transposed(grad_conv, out_ref, t, 1)


def to_spectrum(signal, a_ref, w_ref, turn_ref):
    sources, halves, chans, _ = signal.shape
    n1 = turn_ref.shape[1]
    cos_t, sin_t = turn_ref[0], turn_ref[1]
    by_chan = jnp.swapaxes(signal.reshape(sources * halves, chans, LANES).astype(F32), 0, 1)
    by_chan = by_chan.astype(BF)
    cols = jnp.concatenate([by_chan[i] for i in range(chans)], axis=1)
    first = jnp.dot(a_ref[...], cols, preferred_element_type=F32)
    parts = []
    for i in range(chans):
        y_re = first[:n1, i * LANES : (i + 1) * LANES]
        y_im = first[n1:, i * LANES : (i + 1) * LANES]
        z_re = y_re * cos_t + y_im * sin_t
        z_im = y_im * cos_t - y_re * sin_t
        parts.append(jnp.concatenate([z_re.astype(BF), z_im.astype(BF)], axis=1))
    spec = jnp.dot(jnp.concatenate(parts, axis=0), w_ref[...], preferred_element_type=F32)
    return spec[:, :LANES], spec[:, LANES:]


def from_spectrum(spec, chans, b_ref, wi_ref, turn_ref):
    n1 = turn_ref.shape[1]
    cos_t, sin_t = turn_ref[0], turn_ref[1]
    back = jnp.dot(spec, wi_ref[...], preferred_element_type=F32)
    parts = []
    for i in range(chans):
        u_re = back[i * n1 : (i + 1) * n1, :LANES]
        u_im = back[i * n1 : (i + 1) * n1, LANES:]
        v_re = u_re * cos_t - u_im * sin_t
        v_im = u_im * cos_t + u_re * sin_t
        parts.append(jnp.concatenate([v_re.astype(BF), v_im.astype(BF)], axis=0))
    signal = jnp.dot(b_ref[...], jnp.concatenate(parts, axis=1), preferred_element_type=F32)
    stacked = jnp.stack([signal[:, i * LANES : (i + 1) * LANES] for i in range(chans)], axis=0)
    return jnp.swapaxes(stacked, 0, 1).astype(BF)


def spectral_kernel(
    inv_root, in_ref, a_ref, b_ref, w_ref, wi_ref, turn_ref, streams_ref, filters_ref
):
    sources, _, halves, own, _ = in_ref.shape
    chans = 32
    for first in range(0, own, chans):
        at = slice(first, first + chans)

        def put(out_ref, slot, re, im):
            spec = jnp.concatenate([re.astype(BF), im.astype(BF)], axis=1)
            signal = from_spectrum(spec, chans, b_ref, wi_ref, turn_ref)
            out_ref[:, slot, :, at] = signal.reshape(sources, halves, chans, LANES)

        x_re, x_im = to_spectrum(in_ref[:, 0, :, at], a_ref, w_ref, turn_ref)
        h_re, h_im = to_spectrum(in_ref[:, 2, :, at], a_ref, w_ref, turn_ref)
        put(streams_ref, 0, x_re * h_re - x_im * h_im, x_re * h_im + x_im * h_re)
        g_re, g_im = to_spectrum(in_ref[:, 1, :, at], a_ref, w_ref, turn_ref)
        put(streams_ref, 1, g_re * h_re + g_im * h_im, g_im * h_re - g_re * h_im)
        cross_re = (g_re * x_re + g_im * x_im) * inv_root
        cross_im = (g_im * x_re - g_re * x_im) * inv_root
        put(filters_ref, 0, cross_re, cross_im)


def local_terms(refs, halo_ref, w_ref, in_ref, scratch, t, at):
    q_ref, k_ref, v_ref, cot_ref = refs
    rows = q_ref.shape[0]
    halo = halo_ref[:, at].astype(F32)
    w = w_ref[:, :, at]
    for i, ref in enumerate((q_ref, k_ref, v_ref)):
        stage(scratch[i], ref[:, at], halo[2 * i : 2 * i + 2])
    conv = get_transposed(in_ref, t, 0)
    grad_mixed = get_transposed(in_ref, t, 1)
    grads = (
        cot_ref[:, at].astype(F32) * conv,
        grad_mixed * filter_taps(scratch[2], 8, rows, w, 2),
        grad_mixed * filter_taps(scratch[1], 8, rows, w, 1),
    )
    return w, conv, [grad.astype(BF).astype(F32) for grad in grads]


def sums_kernel(
    q_ref, k_ref, v_ref, cot_ref, halo_ref, w_ref, in_ref, sums_ref, qs, ks, vs
):
    refs = (q_ref, k_ref, v_ref, cot_ref)
    rows = q_ref.shape[0]
    for t, at in enumerate(lane_tiles(q_ref)):
        _, _, grads = local_terms(refs, halo_ref, w_ref, in_ref, (qs, ks, vs), t, at)
        out = []
        for grad, staged in zip(grads, (qs, ks, vs)):
            for lag in range(3):
                out.append(jnp.sum(grad * staged[pl.ds(8 - lag, rows), :], axis=0, keepdims=True))
        out.append(jnp.zeros((1, LANES), F32))
        out.extend(grad[:2] for grad in grads)
        sums_ref[:, at] = jnp.concatenate(out, axis=0).astype(BF)


def finish_kernel(
    q_ref,
    k_ref,
    v_ref,
    cot_ref,
    halo_ref,
    w_ref,
    in_ref,
    out_ref,
    gq_ref,
    gk_ref,
    gv_ref,
    last_ref,
    qs,
    ks,
    vs,
    gs,
):
    refs = (q_ref, k_ref, v_ref, cot_ref)
    rows = q_ref.shape[0]
    gs[pl.ds(rows, 8), :] = jnp.zeros((8, LANES), F32)
    for t, at in enumerate(lane_tiles(q_ref)):
        w, conv, grads = local_terms(refs, halo_ref, w_ref, in_ref, (qs, ks, vs), t, at)
        out_ref[:, at] = (filter_taps(qs, 8, rows, w, 0) * conv).astype(BF)
        for i, (grad, out) in enumerate(zip(grads, (gq_ref, gk_ref, gv_ref))):
            gs[pl.ds(0, rows), :] = grad
            back = w[i, 0:1, :] * grad
            for lag in range(1, 3):
                back = back + w[i, lag : lag + 1, :] * gs[pl.ds(lag, rows), :]
            out[:, at] = back.astype(BF)
            last_ref[i, :, at] = back[rows - 16 :]


def unpack_kernel(in_ref, out_ref):
    for t, at in enumerate(lane_tiles(out_ref)):
        out_ref[:, at] = get_transposed(in_ref, t, 0).astype(BF)


def close_kernel(
    inv_root,
    mine_ref,
    other_ref,
    near_ref,
    last_ref,
    w_ref,
    gq_in,
    gk_in,
    gv_in,
    short_ref,
    gq_out,
    gk_out,
    gv_out,
    short,
    ends,
    sems,
):
    del gq_in, gk_in, gv_in
    mine = mine_ref[...]
    other = other_ref[...].astype(F32)
    total = (mine + other) * inv_root
    ahead = jnp.where(mine > 0.0, other, near_ref[...])
    row = lax.broadcasted_iota(jnp.int32, mine.shape, 0)
    copies = []
    for i, out in enumerate((gq_out, gk_out, gv_out)):
        short[i] = total[3 * i : 3 * i + 3]
        w1 = w_ref[i, 1:2, :]
        w2 = w_ref[i, 2:3, :]
        next0 = ahead[10 + 2 * i : 11 + 2 * i]
        next1 = ahead[11 + 2 * i : 12 + 2 * i]
        last = last_ref[i]
        end1 = last + w1 * next0 + w2 * next1
        fixed = jnp.where(row == 14, last + w2 * next0, jnp.where(row == 15, end1, last))
        ends[i] = fixed.astype(BF)
        copies.append(
            pltpu.make_async_copy(
                ends.at[i], out.at[pl.ds(out.shape[0] - 16, 16), :], sems.at[i]
            )
        )
        copies[-1].start()
    copies.append(pltpu.make_async_copy(short, short_ref, sems.at[3]))
    copies[-1].start()
    for copy in copies:
        copy.wait()


def sum_over_ctx(terms, beside):
    ctx = lax.axis_size("ctx")
    rank = lax.axis_index("ctx")
    slow, fast = rank // 4, rank % 4
    summed = lax.broadcasted_iota(jnp.int32, terms.shape, 0) < 10

    def moved(x, to):
        return lax.ppermute(x.astype(BF), "ctx", [(i, to(i)) for i in range(ctx)]).astype(F32)

    mine = terms.astype(F32)
    near = [moved(mine, lambda i, d=d: i ^ d) for d in (1, 2, 3)]
    total = lax.reduce_precision((mine + near[0]) + (near[1] + near[2]), 8, 7)
    heads = mine
    for d in (1, 2, 3):
        heads = jnp.where(fast == d, near[d - 1], heads)
    beyond = jnp.where(fast == 1, near[2], near[0])
    beyond = jnp.where(fast == 3, 0.0, beyond)
    total = jnp.where(summed, total, heads)
    total, beyond, beside = lax.optimization_barrier((total, beyond, beside))
    far = [moved(total, lambda i, d=d: (i + d) % ctx) for d in (ctx // 4, ctx // 2, 3 * ctx // 4)]
    heads = jnp.where(slow % 2 == 0, far[2], total)
    total = lax.reduce_precision((total + far[1]) + (far[0] + far[2]), 8, 7)
    other = lax.ppermute(
        jnp.where(summed, total, heads).astype(BF), "ctx", [(i, i ^ (ctx // 8)) for i in range(ctx)]
    )
    takes = jnp.where((fast == 3) & (rank < ctx - 1), 1.0, 0.0)
    return jnp.where(summed, total, takes), other, beyond, beside


def params(mib=32):
    return pltpu.CompilerParams(vmem_limit_bytes=mib * 1024 * 1024)


def on_device(query_in, key_in, value_in, cotangent, short_weight, long_filter):
    rows, channels = query_in.shape
    taps = short_weight.shape[1]
    ctx = lax.axis_size("ctx")
    length = rows * ctx
    inv_root = 1.0 / math.sqrt(length)
    own = channels // ctx
    halves = rows // LANES
    outer = length // LANES
    wide_step = 512
    steps = channels // wide_step
    per_step = wide_step // own
    consts = tables(outer, length)

    up = [(i, i + 1) for i in range(ctx - 1)]
    block = lambda: pl.BlockSpec((rows, wide_step), lambda j: (0, j))
    row_block = lambda n: pl.BlockSpec((n, wide_step), lambda j: (0, j))
    w_block = lambda: pl.BlockSpec((3, taps, wide_step), lambda j: (0, 0, j))

    in_vmem = pl.BlockSpec(memory_space=pltpu.VMEM)
    anywhere = pl.BlockSpec(memory_space=pl.ANY)
    tails = pl.pallas_call(
        tails_kernel,
        grid=(1,),
        in_specs=[pl.BlockSpec((16, channels), lambda j: (rows // 16 - 1, 0))] * 3,
        out_specs=pl.BlockSpec((16, channels), lambda j: (0, 0)),
        out_shape=jax.ShapeDtypeStruct((16, channels), BF),
        name="tails",
    )(query_in, key_in, value_in)
    halo = lax.ppermute(tails, "ctx", up)

    buf_shape = jax.ShapeDtypeStruct((ctx, 3, halves, own, LANES), BF)
    packed = pl.pallas_call(
        pack_filter_kernel,
        in_specs=[in_vmem],
        out_specs=in_vmem,
        out_shape=buf_shape,
        compiler_params=params(),
        name="pack_filter",
    )(long_filter)
    packed = pl.pallas_call(
        pack_signals_kernel,
        in_specs=[in_vmem] * 7,
        out_specs=in_vmem,
        out_shape=buf_shape,
        scratch_shapes=[pltpu.VMEM((rows + 8, LANES), F32)] * 3,
        input_output_aliases={6: 0},
        compiler_params=params(),
        name="pack_signals",
    )(query_in, key_in, value_in, cotangent, halo, short_weight, packed)
    arrived = lax.all_to_all(packed, "ctx", split_axis=0, concat_axis=0, tiled=True)

    streams, filters = pl.pallas_call(
        functools.partial(spectral_kernel, inv_root),
        in_specs=[in_vmem] * (1 + len(consts)),
        out_specs=[in_vmem] * 2,
        out_shape=[jax.ShapeDtypeStruct((ctx, n, halves, own, LANES), BF) for n in (2, 1)],
        compiler_params=params(),
        name="spectral",
    )(arrived, *consts)
    streams = lax.all_to_all(streams, "ctx", split_axis=0, concat_axis=0, tiled=True)
    filters = lax.all_to_all(filters, "ctx", split_axis=0, concat_axis=0, tiled=True)

    wide = jax.ShapeDtypeStruct((rows, channels), BF)
    message = pl.BlockSpec((per_step, 2, halves, own, LANES), lambda j: (j, 0, 0, 0, 0))
    local_specs = [block()] * 4 + [row_block(16), w_block(), message]
    local_args = (query_in, key_in, value_in, cotangent, halo, short_weight, streams)
    sums = pl.pallas_call(
        sums_kernel,
        in_specs=[in_vmem] * len(local_args),
        out_specs=in_vmem,
        out_shape=jax.ShapeDtypeStruct((16, channels), BF),
        scratch_shapes=[pltpu.VMEM((rows + 8, LANES), F32)] * 3,
        compiler_params=params(),
        name="sums",
    )(*local_args)
    block_out, grad_q, grad_k, grad_v, last = pl.pallas_call(
        finish_kernel,
        grid=(steps,),
        in_specs=local_specs,
        out_specs=[block()] * 4 + [pl.BlockSpec((3, 16, wide_step), lambda j: (0, 0, j))],
        out_shape=[wide] * 4 + [jax.ShapeDtypeStruct((3, 16, channels), F32)],
        scratch_shapes=[pltpu.VMEM((rows + 8, LANES), F32)] * 4,
        compiler_params=params(),
        name="finish",
    )(*local_args)

    grad_filter = pl.pallas_call(
        unpack_kernel,
        grid=(steps,),
        in_specs=[pl.BlockSpec((per_step, 1, halves, own, LANES), lambda j: (j, 0, 0, 0, 0))],
        out_specs=block(),
        out_shape=wide,
        compiler_params=params(),
        name="unpack_filter",
    )(filters)

    mine, other, beyond, last = sum_over_ctx(sums, last)
    grad_short, grad_q, grad_k, grad_v = pl.pallas_call(
        functools.partial(close_kernel, inv_root),
        in_specs=[in_vmem] * 5 + [anywhere] * 3,
        out_specs=[anywhere] * 4,
        out_shape=[jax.ShapeDtypeStruct((3, taps, channels), F32)] + [wide] * 3,
        scratch_shapes=[
            pltpu.VMEM((3, taps, channels), F32),
            pltpu.VMEM((3, 16, channels), BF),
            pltpu.SemaphoreType.DMA((4,)),
        ],
        input_output_aliases={5: 1, 6: 2, 7: 3},
        compiler_params=params(),
        name="close",
    )(mine, other, beyond, last, short_weight, grad_q, grad_k, grad_v)
    return (block_out, grad_q, grad_k, grad_v, grad_short, grad_filter)


def solution(mesh):
    wide = P("ctx", "tp")
    taps = P(None, None, "tp")
    return jax.shard_map(
        on_device,
        mesh=mesh,
        in_specs=(wide, wide, wide, wide, taps, wide),
        out_specs=(wide, wide, wide, wide, taps, wide),
        check_vma=False,
    )
```
